128 devices in a mesh: dp: 4 (over z), ctx: 8 (over x, core), fsdp: 4 (over y).
Axes of the slice: x: 4, y: 4, z: 4, core: 2. Of those that a mesh axis runs over, the one named last changes fastest.
Arguments:
- tokens: bfloat16 [16, 2048, 576], P(('dp', 'fsdp'), 'ctx'), may hold values from -6 to 6
- pair_order: int32 [16, 8], P(('dp', 'fsdp')), may hold values from 0 to 7, each once within a row
- cotangent: bfloat16 [16, 2048, 576], P(('dp', 'fsdp'), 'ctx'), may hold values from -6 to 6
- norm_first: bfloat16 [2, 576], P(None, 'fsdp'), may hold values from 0.099609375 to 1.8984375
- w_query: bfloat16 [2, 576, 576], P(None, 'fsdp'), may hold values from -0.25 to 0.25
- w_key: bfloat16 [2, 576, 192], P(None, 'fsdp'), may hold values from -0.25 to 0.25
- w_value: bfloat16 [2, 576, 192], P(None, 'fsdp'), may hold values from -0.25 to 0.25
- w_out: bfloat16 [2, 576, 576], P(None, 'fsdp'), may hold values from -3 to 3
- norm_second: bfloat16 [2, 576], P(None, 'fsdp'), may hold values from 0.099609375 to 1.8984375
- w_gate: bfloat16 [2, 576, 1536], P(None, 'fsdp'), may hold values from -0.25 to 0.25
- w_up: bfloat16 [2, 576, 1536], P(None, 'fsdp'), may hold values from -0.25 to 0.25
- w_down: bfloat16 [2, 1536, 576], P(None, 'fsdp'), may hold values from -0.15625 to 0.15625
Outputs:
- mixed: bfloat16 [16, 2048, 576], P(('dp', 'fsdp'), 'ctx')
- grad_tokens: bfloat16 [16, 2048, 576], P(('dp', 'fsdp'), 'ctx')
- grad_norm_first: float32 [2, 576], P(None, 'fsdp')
- grad_w_query: float32 [2, 576, 576], P(None, 'fsdp')
- grad_w_key: float32 [2, 576, 192], P(None, 'fsdp')
- grad_w_value: float32 [2, 576, 192], P(None, 'fsdp')
- grad_w_out: float32 [2, 576, 576], P(None, 'fsdp')
- grad_norm_second: float32 [2, 576], P(None, 'fsdp')
- grad_w_gate: float32 [2, 576, 1536], P(None, 'fsdp')
- grad_w_up: float32 [2, 576, 1536], P(None, 'fsdp')
- grad_w_down: float32 [2, 1536, 576], P(None, 'fsdp')
The draws below stay inside these ranges and needn't reach their ends.
Inputs may be any that keep to these rules, and one draw needn't show every extreme that they name: For sequence s, index r of ctx holds blocks pair_order[s, r] and 15 - pair_order[s, r] of 128 tokens, in this order; each row is a permutation.
All inputs are finite; a program needn't handle non-finite values.
Results may differ from the reference program's by a relative error of at most 0.03.
Values may be sent and summed in bfloat16 or wider, within the bound.
No kernel may reach another device: no remote copies, remote signals or barrier semaphores. Data moves between devices by JAX's collectives and lax.ppermute only.
A program may use at most 128 MiB of HBM per device.

```python
import jax
import jax.numpy as jnp
from jax import lax

D = 576
NH = 9
KVH = 3
HD = 64
FF = 1536
LAYERS = 2
L = 2048
BLK = 128
SEQS = 16
N_CTX = 8


def steps_of(own_key, shape, split, smallest, top_value):
    loudness = 1.0
    for position, blocks in split:
        heights = jax.random.uniform(jax.random.fold_in(jax.random.fold_in(own_key, 6), position), (blocks,), jnp.float32, smallest / len(split), top_value / len(split))
        loudness = loudness * jnp.repeat(jnp.exp(heights), shape[position] // blocks).reshape((-1,) + (1,) * (len(shape) - 1 - position))
    return loudness


def normal_values(rng, dims, width, most, pieces=(), kind=jnp.bfloat16):
    level = steps_of(rng, dims, pieces, -0.22, 0.18) if pieces else 1.0
    array = jax.random.normal(rng, dims, jnp.float32) * width * level
    return jnp.minimum(jnp.maximum(array, -most), most).astype(kind)


def setup_inputs(seed: int = 0) -> dict:
    keys = jax.random.split(jax.random.key(seed), 13)
    return {
        "tokens": normal_values(keys[0], (SEQS, L, D), 1.0, 6.0, ((0, 16), (1, 8))),
        "pair_order": jax.vmap(lambda own: jax.random.permutation(own, N_CTX))(jax.random.split(keys[1], SEQS)).reshape((SEQS, N_CTX)).astype(jnp.int32),
        "cotangent": normal_values(keys[2], (SEQS, L, D), 1.0, 6.0, ((0, 16), (1, 8))),
        "norm_first": jnp.clip(1.0 + 0.18 * jax.random.normal(keys[3], (LAYERS, D), jnp.float32), 0.099609375, 1.8984375).astype(jnp.bfloat16),
        "w_query": normal_values(keys[4], (LAYERS, D, NH * HD), D ** -0.5, 0.25, ((1, 4),)),
        "w_key": normal_values(keys[5], (LAYERS, D, KVH * HD), D ** -0.5, 0.25, ((1, 4),)),
        "w_value": normal_values(keys[6], (LAYERS, D, KVH * HD), D ** -0.5, 0.25, ((1, 4),)),
        "w_out": normal_values(keys[7], (LAYERS, NH * HD, D), 4 ** -0.5, 3.0, ((1, 4),)),
        "norm_second": jnp.clip(1.0 + 0.18 * jax.random.normal(keys[8], (LAYERS, D), jnp.float32), 0.099609375, 1.8984375).astype(jnp.bfloat16),
        "w_gate": normal_values(keys[9], (LAYERS, D, FF), D ** -0.5, 0.25, ((1, 4),)),
        "w_up": normal_values(keys[10], (LAYERS, D, FF), D ** -0.5, 0.25, ((1, 4),)),
        "w_down": normal_values(keys[11], (LAYERS, FF, D), FF ** -0.5, 0.15625, ((1, 4),)),
    }


EPS = 1e-05
THETA = 100000.0
HIGH = lax.Precision.HIGHEST

@jax.custom_vjp
def low(v):
    return lax.optimization_barrier(v.astype(jnp.bfloat16)).astype(jnp.float32)

@jax.custom_vjp
def low_back(v):
    return v

def low_keep(v):
    return (low(v), None)

def low_pass(kept, grad):
    return (grad,)

def back_keep(v):
    return (v, None)

def back_low(kept, grad):
    return (low(grad),)
low.defvjp(low_keep, low_pass)
low_back.defvjp(back_keep, back_low)

def matmul(left, right):
    return jnp.dot(left, right, precision=HIGH, preferred_element_type=jnp.float32)

def rms_scale(resid, gain):
    return resid * lax.rsqrt(lax.optimization_barrier(jnp.mean(resid * resid, axis=-1, keepdims=True)) + EPS) * gain

def rotate(values, cosine, sine):
    half_dim = values.shape[-1] // 2
    turned = jnp.concatenate([-values[..., half_dim:], values[..., :half_dim]], axis=-1)
    return values * cosine + turned * sine

def positions(pair_row):
    slot_ids = jnp.arange(L, dtype=jnp.int32)
    owner_rank = slot_ids // (2 * BLK)
    offset_in = slot_ids % (2 * BLK)
    pair_id = pair_row[owner_rank]
    return jnp.where(offset_in < BLK, pair_id * BLK + offset_in, (2 * N_CTX - 1 - pair_id) * BLK + offset_in - BLK)

def tables(pos_table):
    freq_index = jnp.arange(HD // 2, dtype=jnp.float32)
    freq_rate = jnp.power(THETA, -2.0 * freq_index / HD)
    angle = pos_table.astype(jnp.float32)[:, None] * freq_rate[None, :]
    cosine = jnp.cos(angle)
    sine = jnp.sin(angle)
    return (jnp.concatenate([cosine, cosine], axis=-1), jnp.concatenate([sine, sine], axis=-1))

def forward_one(resid, weights, cosine, sine, allowed):
    group_size = NH // KVH
    scale = HD ** (-0.5)
    for layer_idx in range(LAYERS):
        gain_first, query_w, key_w, value_w, out_w, gain_second, gate_w, up_w, down_w = [item[layer_idx] for item in weights]
        normed = low(rms_scale(resid, gain_first))
        query_rows = low(rotate(low_back(matmul(normed, query_w)).reshape(L, NH, HD), cosine, sine))
        key_rows = low(rotate(low_back(matmul(normed, key_w)).reshape(L, KVH, HD), cosine, sine))
        value_rows = low(low_back(matmul(normed, value_w))).reshape(L, KVH, HD)
        query_rows = query_rows.reshape(L, KVH, group_size, HD)
        raw_score = jnp.einsum('qhgd,khd->hgqk', query_rows, key_rows, precision=HIGH) * scale
        score = jnp.where(allowed, low_back(raw_score), -1e+30)
        prob = low(jax.nn.softmax(score, axis=-1))
        heads_out = jnp.einsum('hgqk,khd->qhgd', prob, value_rows, precision=HIGH).reshape(L, NH * HD)
        attn_rows = low(low_back(heads_out))
        middle = resid + low_back(matmul(attn_rows, out_w))
        normed_two = low(rms_scale(middle, gain_second))
        gate_act = low_back(matmul(normed_two, gate_w))
        up_proj = low_back(matmul(normed_two, up_w))
        hidden = low(jax.nn.silu(gate_act) * up_proj)
        resid = middle + low_back(matmul(hidden, down_w))
    return resid

def reference(tokens, pair_order, cotangent, norm_first, w_query, w_key, w_value, w_out, norm_second, w_gate, w_up, w_down):
    params = tuple((item.astype(jnp.float32) for item in (norm_first, w_query, w_key, w_value, w_out, norm_second, w_gate, w_up, w_down)))

    def forward(inputs, weights):

        def one_sequence(items):
            rows_in, pair_row = items
            pos_table = positions(pair_row)
            cosine, sine = tables(pos_table)
            allowed = pos_table[None, :] <= pos_table[:, None]
            return forward_one(rows_in, weights, cosine[:, None, :], sine[:, None, :], allowed)
        return lax.map(jax.checkpoint(one_sequence), (inputs, pair_order))
    outputs, pull_back = jax.vjp(forward, tokens.astype(jnp.float32), params)
    grad_in, grad_params = pull_back(cotangent.astype(jnp.float32))
    return (outputs.astype(jnp.bfloat16), grad_in.astype(jnp.bfloat16), grad_params[0], grad_params[1], grad_params[2], grad_params[3], grad_params[4], grad_params[5], grad_params[6], grad_params[7], grad_params[8])
```

```python
import jax
import jax.numpy as jnp
from jax import lax
from jax.experimental import pallas as pl
from jax.experimental.pallas import tpu as pltpu
from jax.sharding import PartitionSpec as P

NH = 9
KVH = 3
HD = 64
LAYERS = 2
D = 576
FF = 1536
HALF = 768
EPS = 1e-05
THETA = 100000.0
NEG = -1e30
BF = jnp.bfloat16
F32 = jnp.float32
CROWS = 160
MROWS = 480
VMEM_LIMIT = 60 * 1024 * 1024

ANY = pl.BlockSpec(memory_space=pl.ANY)
VM = pl.BlockSpec(memory_space=pltpu.VMEM)
SM = pl.BlockSpec(memory_space=pltpu.SMEM)


def nt(a, b):
    return lax.dot_general(a, b, (((1,), (1,)), ((), ())), preferred_element_type=F32)


def nn(a, b):
    return jnp.dot(a, b, preferred_element_type=F32)


def shaped(shape, dtype):
    return jax.ShapeDtypeStruct(shape, dtype)


def call(kernel, ins, specs, outs, scratch, flops, nbytes):
    return pl.pallas_call(
        kernel,
        out_shape=outs,
        in_specs=specs,
        out_specs=[VM] * len(outs),
        scratch_shapes=scratch,
        compiler_params=pltpu.CompilerParams(vmem_limit_bytes=VMEM_LIMIT),
        cost_estimate=pl.CostEstimate(flops=1000, bytes_accessed=1000, transcendentals=0),
    )(*ins)


PIECES = 7


def unit_copies(sc, pieces, row, rows, dst, stride, split_rows, sems, first):
    core = sc[1]
    copies = []

    def add(src, slot, half):
        if split_rows:
            at = pl.multiple_of(slot * stride + half * (stride // 2), 16)
            target = dst.at[pl.ds(at, rows)]
        else:
            lanes = pl.ds(pl.multiple_of(half * HALF, 128), HALF)
            target = dst.at[pl.ds(pl.multiple_of(slot * stride, 16), rows), lanes]
        copies.append(pltpu.make_async_copy(src, target, sems.at[first + len(copies)]))

    for half in range(2):
        add(pieces[0].at[half, pl.ds(row, rows)], sc[0], half)
    for k in range(3):
        slot = lax.rem(sc[0] + k + 1, 4)
        add(pieces[1 + k].at[pl.ds(row, rows)], slot, core)
        add(pieces[4 + k].at[pl.ds(row, rows)], slot, 1 - core)
    for copy in copies:
        copy.start()
    return copies


def wait_all(copies):
    for copy in copies:
        copy.wait()


def lane_low(shape):
    return lax.rem(lax.broadcasted_iota(jnp.int32, shape, 1), 64) < 32


def rope(values, cosine, sine):
    width = values.shape[1]
    up = pltpu.roll(values, width - 32, 1)
    down = pltpu.roll(values, 32, 1)
    return values * cosine + jnp.where(lane_low(values.shape), -up, down) * sine


def rope_back(values, cosine, sine):
    width = values.shape[1]
    spun = values * sine
    up = pltpu.roll(spun, width - 32, 1)
    down = pltpu.roll(spun, 32, 1)
    return values * cosine + jnp.where(lane_low(values.shape), up, -down)


def table_lanes(narrow, kv_fill):
    first = lax.broadcasted_iota(jnp.int32, narrow.shape, 1) < HD
    pair = jnp.where(first, narrow, kv_fill)
    return jnp.concatenate([pair] * 3 + [narrow] * 4 + [jnp.where(first, narrow, 0.0)], axis=1)


def norm_factor(rows):
    return lax.rsqrt(jnp.mean(rows * rows, axis=-1, keepdims=True) + EPS)


def norm_back(rows, gain, upstream):
    factor = norm_factor(rows)
    scaled = upstream * gain
    inner = jnp.mean(scaled * rows, axis=-1, keepdims=True)
    grad_in = factor * scaled - rows * (factor * factor * factor) * inner
    return grad_in, jnp.sum(upstream * rows * factor, axis=0, keepdims=True)


def project_kernel(at, sc, x, gain, cosine, sine, *refs):
    pieces, (kv, q, normed_out, weight, sems) = refs[:PIECES], refs[PIECES:]
    copies = unit_copies(sc, pieces, at, 144, weight, 144, False, sems, 0)
    rows = x[...]
    normed = (rows * norm_factor(rows) * gain[...]).astype(BF)
    normed_out[...] = normed
    wait_all(copies)
    raw = nn(normed, weight[:, :1024])
    turned = rope(raw, table_lanes(cosine[...], 1.0), table_lanes(sine[...], 0.0))
    for s in range(8):
        kv[s, 0] = turned[:128, :384].astype(BF)
        kv[s, 1] = turned[128:, :384].astype(BF)
    q[...] = (turned[:, 384:960] * (HD**-0.5)).astype(BF)


def project(sc, x, gain, tables, pieces):
    pieces, at = pieces

    def kernel(*refs):
        project_kernel(at, *refs)

    return call(
        kernel,
        (sc, x, gain, *tables, *pieces),
        [SM] + [VM] * 4 + [ANY] * PIECES,
        (shaped((8, 2, 128, 384), BF), shaped((256, D), BF), shaped((256, D), BF)),
        [pltpu.VMEM((D, FF), BF), pltpu.SemaphoreType.DMA((8,))],
        2 * 256 * D * 960,
        5_000_000,
    )


def fill_padded(target, rows, first_row, first_lane):
    for g in range(KVH):
        for b in range(2):
            for h in range(3):
                head = 3 * g + h
                piece = rows[128 * b : 128 * b + 128, 64 * head : 64 * head + 64]
                zero = jnp.zeros_like(piece)
                pair = (piece, zero) if first_lane == 0 else (zero, piece)
                target[2 * g + b, first_row + 128 * h : first_row + 128 * h + 128] = (
                    jnp.concatenate(pair, axis=1).astype(BF)
                )


def slot_of(sc, i):
    pair = sc[2]
    is_low = i <= pair
    rank = jnp.where(is_low, sc[4 + jnp.minimum(i, 7)], sc[4 + jnp.maximum(8 - i + pair, 0) % 8])
    block = 2 * rank + jnp.where(is_low, 0, 1)
    return is_low, block


def triangle(always):
    key_at = lax.broadcasted_iota(jnp.int32, (128, 384), 0)
    query_at = lax.rem(lax.broadcasted_iota(jnp.int32, (128, 384), 1), 128)
    return jnp.logical_or(key_at <= query_at, always)


def attend_kernel(sc, q, held, out, log_total, padded, acc, tops, totals):
    fill_padded(padded, q[...].astype(F32), 0, 0)
    acc[...] = jnp.zeros_like(acc)
    tops[...] = jnp.full_like(tops, NEG)
    totals[...] = jnp.zeros_like(totals)

    def update(state, block, query_block, allowed):
        for g in range(KVH):
            tile = held[block, :, 128 * g : 128 * g + 128]
            score = nt(tile, padded[2 * g + query_block])
            if allowed is not None:
                score = jnp.where(allowed, score, NEG)
            at = 3 * state + g
            top = tops[at, 0:1]
            new_top = jnp.maximum(top, jnp.max(score, axis=0, keepdims=True))
            shrink = jnp.exp(top - new_top)
            expo = jnp.exp(score - new_top)
            tops[at, 0:1] = new_top
            totals[at, 0:1] = totals[at, 0:1] * shrink + jnp.sum(expo, axis=0, keepdims=True)
            turned = tile.astype(F32).T[64:].astype(BF)
            acc[at] = acc[at] * shrink + nn(turned, expo.astype(BF))

    def step(i, carry):
        update(2, 2 * sc[4 + i], 1, None)
        is_low, block = slot_of(sc, i)
        which = jnp.where(is_low, 0, 1)
        update(which, block, which, triangle(i != sc[2]))
        return carry

    lax.fori_loop(0, 8, step, 0)
    update(1, 2 * sc[3] + 1, 1, triangle(False))
    for g in range(KVH):
        for b in range(2):
            if b == 0:
                top, total, rows = tops[g, 0:1], totals[g, 0:1], acc[g]
            else:
                top_a, top_b = tops[3 + g, 0:1], tops[6 + g, 0:1]
                top = jnp.maximum(top_a, top_b)
                left, right = jnp.exp(top_a - top), jnp.exp(top_b - top)
                total = totals[3 + g, 0:1] * left + totals[6 + g, 0:1] * right
                rows = acc[3 + g] * left + acc[6 + g] * right
            log_total[2 * g + b, 0:1] = top + jnp.log(total)
            heads = (rows / total).T
            for h in range(3):
                head = 3 * g + h
                out[128 * b : 128 * b + 128, 64 * head : 64 * head + 64] = heads[
                    128 * h : 128 * h + 128
                ].astype(BF)


def attend(sc, q, kvs):
    return call(
        attend_kernel,
        (sc, q, kvs),
        [SM, VM, VM],
        (shaped((256, D), BF), shaped((6, 8, 384), F32)),
        [
            pltpu.VMEM((6, 384, 128), BF),
            pltpu.VMEM((9, 64, 384), F32),
            pltpu.VMEM((9, 8, 384), F32),
            pltpu.VMEM((9, 8, 384), F32),
        ],
        4 * 17 * 3 * 128 * 128 * 384,
        4_000_000,
    )


def attend_back_kernel(
    sc, q, rows_out, grad_out, log_total, cosine, sine, held, grad_q, grad_kv, both, delta, acc,
    dkv, dq,
):
    fill_padded(both, q[...].astype(F32), 0, 0)
    fill_padded(both, grad_out[...].astype(F32), 384, 64)
    product = rows_out[...].astype(F32) * grad_out[...].astype(F32)
    for g in range(KVH):
        for b in range(2):
            for h in range(3):
                head = 3 * g + h
                piece = product[128 * b : 128 * b + 128, 64 * head : 64 * head + 64]
                delta[2 * g + b, 0:1, 128 * h : 128 * h + 128] = jnp.sum(
                    piece.T, axis=0, keepdims=True
                )
    acc[...] = jnp.zeros_like(acc)
    dkv[...] = jnp.zeros_like(dkv)

    def update(block, query_block, allowed):
        for g in range(KVH):
            lanes = slice(128 * g, 128 * g + 128)
            tile = held[block, :, lanes]
            at = 2 * g + query_block
            score = nt(tile, both[at, :384])
            if allowed is not None:
                score = jnp.where(allowed, score, NEG)
            prob = jnp.exp(score - log_total[at, 0:1])
            grad_prob = nt(tile, both[at, 384:])
            grad_score = (prob * (grad_prob - delta[at, 0:1])).astype(BF)
            turned = tile.astype(F32).T[:64].astype(BF)
            acc[at] = acc[at] + nn(turned, grad_score)
            pair = jnp.concatenate([grad_score, prob.astype(BF)], axis=1)
            dkv[block, :, lanes] = dkv[block, :, lanes] + nn(pair, both[at])

    def step(i, carry):
        update(2 * sc[4 + i], 1, None)
        is_low, block = slot_of(sc, i)
        update(block, jnp.where(is_low, 0, 1), triangle(i != sc[2]))
        return carry

    lax.fori_loop(0, 8, step, 0)
    update(2 * sc[3] + 1, 1, triangle(False))
    dq[...] = jnp.zeros_like(dq)
    for g in range(KVH):
        for b in range(2):
            heads = acc[2 * g + b].T
            for h in range(3):
                head = 3 * g + h
                dq[128 * b : 128 * b + 128, 64 * head : 64 * head + 64] = heads[
                    128 * h : 128 * h + 128
                ] * (HD**-0.5)
    turned = rope_back(
        dq[...], table_lanes(cosine[...], 1.0)[:, 384:], table_lanes(sine[...], 0.0)[:, 384:]
    )
    grad_q[...] = turned[:, :D].astype(BF)
    for block in range(16):
        grad_kv[block] = dkv[block].astype(BF)


def attend_back(sc, q, rows_out, grad_out, log_total, tables, kvs):
    return call(
        attend_back_kernel,
        (sc, q, rows_out, grad_out, log_total, *tables, kvs),
        [SM] + [VM] * 7,
        (shaped((256, D), BF), shaped((16, 128, 384), BF)),
        [
            pltpu.VMEM((6, 768, 128), BF),
            pltpu.VMEM((6, 8, 384), F32),
            pltpu.VMEM((6, 64, 384), F32),
            pltpu.VMEM((16, 128, 384), F32),
            pltpu.VMEM((256, 640), F32),
        ],
        10 * 17 * 3 * 128 * 128 * 384,
        8_000_000,
    )


CHUNK = 512


def feed_kernel(sc, x, rows_out, gain, at_c, at_m, *refs):
    c_pieces, m_pieces, refs = refs[:PIECES], refs[PIECES : 2 * PIECES], refs[2 * PIECES :]
    middle_out, normed_out, gate_out, up_out, after = refs[:5]
    weight, gate_w, up_w, down_w, sems = refs[5:]
    first = unit_copies(sc, c_pieces, at_c, 144, weight, 144, False, sems, 0)
    second = unit_copies(sc, m_pieces, at_m, 144, gate_w, 144, False, sems, 8)
    second += unit_copies(sc, m_pieces, at_m + 144, 144, up_w, 144, False, sems, 16)
    third = unit_copies(sc, m_pieces, at_m + 288, 192, down_w, 384, True, sems, 24)
    wait_all(first)
    middle = x[...] + nn(rows_out[...], weight[:, 960:])
    middle_out[...] = middle
    normed = (middle * norm_factor(middle) * gain[...]).astype(BF)
    normed_out[...] = normed
    wait_all(second)
    wait_all(third)
    total = middle
    for at in range(0, FF, CHUNK):
        gate = nn(normed, gate_w[:, at : at + CHUNK])
        up = nn(normed, up_w[:, at : at + CHUNK])
        gate_out[:, at : at + CHUNK] = gate
        up_out[:, at : at + CHUNK] = up
        hidden = (gate * jax.nn.sigmoid(gate) * up).astype(BF)
        total = total + nn(hidden, down_w[at : at + CHUNK, :D])
    after[...] = total


def feed(sc, x, rows_out, gain, c_pieces, m_pieces):
    (c_pieces, at_c), (m_pieces, at_m) = c_pieces, m_pieces

    def kernel(sc, x, rows_out, gain, *refs):
        return feed_kernel(sc, x, rows_out, gain, at_c, at_m, *refs)

    wide = shaped((256, FF), F32)
    narrow = shaped((256, D), F32)
    return call(
        kernel,
        (sc, x, rows_out, gain, *c_pieces, *m_pieces),
        [SM] + [VM] * 3 + [ANY] * 2 * PIECES,
        (narrow, shaped((256, D), BF), wide, wide, narrow),
        [
            pltpu.VMEM((D, FF), BF),
            pltpu.VMEM((D, FF), BF),
            pltpu.VMEM((D, FF), BF),
            pltpu.VMEM((FF, HALF), BF),
            pltpu.SemaphoreType.DMA((32,)),
        ],
        2 * 256 * D * (D + 3 * FF),
        14_000_000,
    )


def feed_back_kernel(sc, upstream, middle, gate, up, gain, at_c, at_m, *refs):
    c_pieces, m_pieces, refs = refs[:PIECES], refs[PIECES : 2 * PIECES], refs[2 * PIECES :]
    grad_middle, grad_attn_out, grad_rows, grad_gate_out, grad_up_out, hidden_out, grad_gain = refs[
        :7
    ]
    weight, gate_w, up_w, down_w, sems = refs[7:]
    third = unit_copies(sc, m_pieces, at_m + 288, 192, down_w, 384, True, sems, 24)
    second = unit_copies(sc, m_pieces, at_m, 144, gate_w, 144, False, sems, 8)
    second += unit_copies(sc, m_pieces, at_m + 144, 144, up_w, 144, False, sems, 16)
    first = unit_copies(sc, c_pieces, at_c, 144, weight, 144, False, sems, 0)
    grad_down = upstream[...].astype(BF)
    wait_all(third)
    wait_all(second)
    grad_normed = jnp.zeros((256, D), F32)
    for at in range(0, FF, CHUNK):
        lanes = slice(at, at + CHUNK)
        grad_hidden = nt(grad_down, down_w[at : at + CHUNK, :D])
        gate_act, up_proj = gate[:, lanes], up[:, lanes]
        sigma = jax.nn.sigmoid(gate_act)
        silu = gate_act * sigma
        grad_gate = (grad_hidden * up_proj * sigma * (1.0 + gate_act * (1.0 - sigma))).astype(BF)
        grad_up = (grad_hidden * silu).astype(BF)
        grad_gate_out[:, lanes] = grad_gate
        grad_up_out[:, lanes] = grad_up
        hidden_out[:, lanes] = (silu * up_proj).astype(BF)
        grad_normed = grad_normed + nt(grad_gate, gate_w[:, lanes]) + nt(grad_up, up_w[:, lanes])
    back, grad_gain_sum = norm_back(middle[...], gain[...], grad_normed)
    grad_gain[...] = grad_gain_sum
    total = upstream[...] + back
    grad_middle[...] = total
    grad_attn = total.astype(BF)
    grad_attn_out[...] = grad_attn
    wait_all(first)
    grad_rows[...] = nt(grad_attn, weight[:, 960:]).astype(BF)


def feed_back(sc, upstream, middle, gate, up, gain, c_pieces, m_pieces):
    (c_pieces, at_c), (m_pieces, at_m) = c_pieces, m_pieces

    def kernel(sc, upstream, middle, gate, up, gain, *refs):
        return feed_back_kernel(sc, upstream, middle, gate, up, gain, at_c, at_m, *refs)

    wide = shaped((256, FF), BF)
    return call(
        kernel,
        (sc, upstream, middle, gate, up, gain, *c_pieces, *m_pieces),
        [SM] + [VM] * 5 + [ANY] * 2 * PIECES,
        (
            shaped((256, D), F32),
            shaped((256, D), BF),
            shaped((256, D), BF),
            wide,
            wide,
            wide,
            shaped((1, D), F32),
        ),
        [
            pltpu.VMEM((D, FF), BF),
            pltpu.VMEM((D, FF), BF),
            pltpu.VMEM((D, FF), BF),
            pltpu.VMEM((FF, HALF), BF),
            pltpu.SemaphoreType.DMA((32,)),
        ],
        2 * 256 * D * (D + 3 * FF),
        14_000_000,
    )


def store_piece(sc, keep, send, owner, half, rows, value, own_first=True):
    owner = lax.rem(owner - sc[0] + 4, 4) if own_first else owner

    @pl.when(sc[1] == half)
    def _():
        keep[owner, rows] = value

    @pl.when(sc[1] != half)
    def _():
        send[owner, rows] = value


def feed_grads_kernel(sc, normed, grad_gate, grad_up, hidden, upstream, keep, send, turned, tall):
    turned[...] = normed[...].astype(F32).T.astype(BF)
    for at in range(0, FF, CHUNK):
        tall[at : at + CHUNK] = hidden[:, at : at + CHUNK].astype(F32).T.astype(BF)
    grad_down = jnp.concatenate(
        [upstream[...], jnp.zeros((256, HALF - D), F32)], axis=1
    ).astype(BF)
    for half in range(2):
        lanes = slice(HALF * half, HALF * half + HALF)
        for owner in range(4):
            left = turned[144 * owner : 144 * owner + 144]
            store_piece(
                sc, keep, send, owner, half, slice(0, 144), nn(left, grad_gate[:, lanes]).astype(BF)
            )
            store_piece(
                sc, keep, send, owner, half, slice(144, 288), nn(left, grad_up[:, lanes]).astype(BF)
            )
            at = 384 * owner + 192 * half
            store_piece(
                sc,
                keep,
                send,
                owner,
                half,
                slice(288, 480),
                nn(tall[at : at + 192], grad_down).astype(BF),
            )


def feed_grads(sc, normed, grad_gate, grad_up, hidden, upstream):
    out = shaped((4, MROWS, HALF), BF)
    return call(
        feed_grads_kernel,
        (sc, normed, grad_gate, grad_up, hidden, upstream),
        [SM] + [VM] * 5,
        (out, out),
        [pltpu.VMEM((D, 256), BF), pltpu.VMEM((FF, 256), BF)],
        2 * 256 * D * 3 * FF,
        9_000_000,
    )


def grad_kv_rows(grad_kvs, cosine, sine, half):
    total = grad_kvs[0, half].astype(F32)
    for r in range(1, 8):
        total = total + grad_kvs[r, half].astype(F32)
    rows = slice(128 * half, 128 * half + 128)
    cos_t, sin_t = table_lanes(cosine[rows], 1.0), table_lanes(sine[rows], 0.0)
    return rope_back(total, cos_t[:, :384], sin_t[:, :384])


def project_back_kernel(
    at, sc, x, gain, cosine, sine, grad_middle, grad_q, normed, attn_rows, grad_attn, gain_two,
    grad_kvs, *refs,
):
    pieces, (upstream, keep, send, weight, buf, turned, sems) = refs[:PIECES], refs[PIECES:]
    copies = unit_copies(sc, pieces, at, 144, weight, 144, False, sems, 0)
    for half in range(2):
        rows = slice(128 * half, 128 * half + 128)
        buf[rows, :384] = grad_kv_rows(grad_kvs, cosine, sine, half)
    buf[:, 384:960] = grad_q[...].astype(F32)
    buf[:, 960:] = grad_attn[...].astype(F32)
    inner = buf[:, :960].astype(BF)
    wait_all(copies)
    grad_normed = nt(inner, weight[:, :960])
    back, grad_gain = norm_back(x[...], gain[...], grad_normed)
    upstream[...] = grad_middle[...] + back
    turned[0] = normed[...].astype(F32).T.astype(BF)
    turned[1] = attn_rows[...].astype(F32).T.astype(BF)
    right = [buf[:, :HALF].astype(BF), buf[:, HALF:].astype(BF)]
    lane = lax.broadcasted_iota(jnp.int32, (144, HALF), 1)
    gains = (grad_gain, gain_two[...])
    for owner in range(4):
        rows = slice(144 * owner, 144 * owner + 144)
        for half in range(2):
            value = nn(turned[0, rows], right[half])
            if half == 1:
                value = jnp.where(lane < 192, value, nn(turned[1, rows], right[1]))
            store_piece(sc, keep, send, owner, half, slice(0, 144), value.astype(BF))
            row = jnp.concatenate([gains[half][:, rows], jnp.zeros((1, HALF - 144), F32)], axis=1)
            block = jnp.broadcast_to(row, (16, HALF))
            store_piece(sc, keep, send, owner, half, slice(144, 160), block.astype(BF))


def project_back(
    sc, x, gain, tables, grad_middle, grad_q, normed, attn_rows, grad_attn, gain_two, grad_kvs, pieces
):
    out = shaped((4, CROWS, HALF), BF)
    pieces, at = pieces

    def kernel(*refs):
        project_back_kernel(at, *refs)

    return call(
        kernel,
        (
            sc, x, gain, *tables, grad_middle, grad_q, normed, attn_rows, grad_attn, gain_two,
            grad_kvs, *pieces,
        ),
        [SM] + [VM] * 11 + [ANY] * PIECES,
        (shaped((256, D), F32), out, out),
        [
            pltpu.VMEM((D, FF), BF),
            pltpu.VMEM((256, FF), F32),
            pltpu.VMEM((2, D, 256), BF),
            pltpu.SemaphoreType.DMA((8,)),
        ],
        2 * 256 * D * (960 + FF),
        10_000_000,
    )


def early_grads_kernel(sc, normed, grad_q, attn_rows, grad_attn, keep, send, turned):
    turned[0] = normed[...].astype(F32).T.astype(BF)
    turned[1] = attn_rows[...].astype(F32).T.astype(BF)
    for half, right in enumerate((grad_q, grad_attn)):
        for owner in range(4):
            value = nn(turned[half, 144 * owner : 144 * owner + 144], right[...])
            value = jnp.concatenate([value, jnp.zeros((144, HALF - D), F32)], axis=1)
            value = jnp.concatenate([value, jnp.zeros((16, HALF), F32)], axis=0)
            store_piece(sc, keep, send, owner, half, slice(0, CROWS), value.astype(BF))


def early_grads(sc, normed, grad_q, attn_rows, grad_attn):
    out = shaped((4, CROWS, HALF), BF)
    return call(
        early_grads_kernel,
        (sc, normed, grad_q, attn_rows, grad_attn),
        [SM] + [VM] * 4,
        (out, out),
        [pltpu.VMEM((2, D, 256), BF)],
        4 * 256 * D * D,
        4_000_000,
    )


LROWS = 80


def late_back_kernel(
    at, sc, x, gain, cosine, sine, grad_middle, grad_q, normed, gain_two, grad_kvs, *refs
):
    pieces, (grad_tokens, keep, send, weight, buf, turned, sems) = refs[:PIECES], refs[PIECES:]
    copies = unit_copies(sc, pieces, at, 144, weight, 144, False, sems, 0)
    for half in range(2):
        rows = slice(128 * half, 128 * half + 128)
        buf[rows, :384] = grad_kv_rows(grad_kvs, cosine, sine, half).astype(BF)
    buf[:, 384:] = grad_q[...]
    wait_all(copies)
    grad_normed = nt(buf[...], weight[:, :960])
    back, grad_gain = norm_back(x[...], gain[...], grad_normed)
    grad_tokens[...] = (grad_middle[...] + back).astype(BF)
    turned[...] = normed[...].astype(F32).T.astype(BF)
    gains = (grad_gain, gain_two[...])
    for owner in range(4):
        rows = slice(144 * owner, 144 * owner + 144)
        value = nn(turned[rows], buf[:, :384])
        for half in range(2):
            row = jnp.concatenate([gains[half][:, rows], jnp.zeros((1, 384 - 144), F32)], axis=1)
            block = jnp.broadcast_to(row, (8, 384))
            piece = jnp.concatenate([value[72 * half : 72 * half + 72], block], axis=0)
            store_piece(sc, keep, send, owner, half, slice(0, LROWS), piece.astype(BF), False)


def late_back(sc, x, gain, tables, grad_middle, grad_q, normed, gain_two, grad_kvs, pieces):
    out = shaped((4, LROWS, 384), BF)
    pieces, at = pieces

    def kernel(*refs):
        late_back_kernel(at, *refs)

    return call(
        kernel,
        (sc, x, gain, *tables, grad_middle, grad_q, normed, gain_two, grad_kvs, *pieces),
        [SM] + [VM] * 9 + [ANY] * PIECES,
        (shaped((256, D), BF), out, out),
        [
            pltpu.VMEM((D, FF), BF),
            pltpu.VMEM((256, 960), BF),
            pltpu.VMEM((D, 256), BF),
            pltpu.SemaphoreType.DMA((8,)),
        ],
        2 * 256 * D * (960 + 384),
        6_000_000,
    )


def in_order(sc, mine, other):
    rows = mine[...].astype(F32), other[...].astype(F32)
    is_first = sc[1] == 0
    return jnp.where(is_first, rows[0], rows[1]), jnp.where(is_first, rows[1], rows[0])


def heads_apart(rows):
    keys = [rows[:, 128 * g : 128 * g + HD] for g in range(KVH)]
    values = [rows[:, 128 * g + HD : 128 * g + 128] for g in range(KVH)]
    return jnp.concatenate(keys, axis=1), jnp.concatenate(values, axis=1)


def place_all(pairs, sems, layer):
    copies = [
        pltpu.make_async_copy(src, dst.at[layer], sems.at[k]) for k, (src, dst) in enumerate(pairs)
    ]
    for copy in copies:
        copy.start()
    wait_all(copies)


def fill_wide(left, right, gate, up, down):
    gate[:, :HALF], gate[:, HALF:] = left[:144], right[:144]
    up[:, :HALF], up[:, HALF:] = left[144:288], right[144:288]
    down[:192], down[192:] = left[288:, :D], right[288:, :D]


def assemble_last_kernel(sc, mine, other, *refs):
    outs, held, sems = refs[:3], refs[3:6], refs[6]
    fill_wide(*in_order(sc, mine, other), *held)
    place_all(zip(held, outs), sems, 1)


def assemble_first_kernel(sc, mine, other, *refs):
    outs, held, sems = refs[3:12], refs[12:21], refs[21]
    left, right = in_order(sc, mine, other)
    fill_wide(left[CROWS:], right[CROWS:], *held[:3])
    query, out, key, value, gain_a, gain_b = held[3:]
    query[:, :384], query[:, 384:] = left[:144, 384:], right[:144, :192]
    out[...] = right[:144, 192:]
    key[...], value[...] = heads_apart(left[:144, :384])
    gain_a[...], gain_b[...] = left[144:152, :256], right[144:152, :256]
    place_all(zip(held[:3], outs[:3]), sems, 0)
    place_all(zip(held[3:], outs[3:]), sems, 1)


def assemble_rest_kernel(sc, early_mine, early_other, late_mine, late_other, *refs):
    outs, held, sems = refs[6:12], refs[12:18], refs[18]
    query, out, key, value, gain_a, gain_b = held
    left, right = in_order(sc, early_mine, early_other)
    query[...], out[...] = left[:144, :D], right[:144, :D]
    left, right = in_order(sc, late_mine, late_other)
    key[...], value[...] = heads_apart(jnp.concatenate([left[:72], right[:72]], axis=0))
    gain_a[...], gain_b[...] = left[72:80, :256], right[72:80, :256]
    place_all(zip(held, outs), sems, 0)


PLACED = (
    ((144, FF),) * 2 + ((384, D),) + ((144, D),) * 2 + ((144, KVH * HD),) * 2 + ((8, 256),) * 2
)


def assemble(kernel, ins, before, shapes, apart=()):
    outs = tuple(shaped((LAYERS,) + shape, F32) for shape in shapes)
    scratch = [pltpu.VMEM(shape, F32) for shape in shapes]
    made = pl.pallas_call(
        kernel,
        out_shape=outs,
        in_specs=[SM] + [VM] * (len(ins) - 1) + [ANY] * len(before),
        out_specs=[ANY] * len(outs),
        scratch_shapes=scratch + [pltpu.SemaphoreType.DMA((len(shapes),))],
        input_output_aliases={len(ins) + k: k for k in range(len(before))},
        compiler_params=pltpu.CompilerParams(vmem_limit_bytes=VMEM_LIMIT),
        cost_estimate=pl.CostEstimate(flops=1000, bytes_accessed=1000, transcendentals=0),
    )(*ins, *before)
    return tuple(apart) + tuple(made)


def ring(axis, shift):
    n = lax.axis_size(axis)
    return [(i, (i + shift) % n) for i in range(n)]


def swap_core(value):
    return lax.ppermute(value, "core", [(0, 1), (1, 0)])


def all_pairs(value, axis):
    return lax.all_to_all(value, axis, 0, 0, tiled=True)


def copied(value, n):
    return jnp.broadcast_to(value[None], (n,) + value.shape)


def added(parts):
    total = parts[0].astype(F32)
    for part in parts[1:]:
        total = total + part.astype(F32)
    return total


def summed_rows(pieces, n):
    return added([pieces[k] for k in range(n)])


def around(own, axis):
    own = own.astype(BF)
    return added([own] + [lax.ppermute(own, axis, ring(axis, s)) for s in (1, 2, 3)])


def phase(*values):
    return lax.optimization_barrier(values)


def sent(pieces, shifts):
    return [lax.ppermute(pieces[k], "fsdp", ring("fsdp", k)) for k in shifts]


def near(mine, shifts):
    return [lax.ppermute(mine, "fsdp", ring("fsdp", -k)) for k in shifts]


def swap_all(parts):
    return [swap_core(part) for part in parts]


def joined(parts):
    return [
        jnp.concatenate([added([keep[k], got[k]]).astype(BF) for keep, got in parts], axis=0)
        for k in range(4)
    ]


def quarters(total):
    return total.astype(BF).reshape(4, -1, HALF)


def halves_of(full):
    return jnp.stack([full[:, :HALF], full[:, HALF:]])


def of_core(own, core):
    return lax.dynamic_index_in_dim(own, core, 0, keepdims=False)


def local(
    tokens, pair_order, cotangent, norm_first, w_query, w_key, w_value, w_out, norm_second,
    w_gate, w_up, w_down,
):
    core = lax.axis_index("core")
    rank = lax.axis_index("x") * 2 + core
    y = lax.axis_index("fsdp")
    order = pair_order[0]
    my_pair = lax.dynamic_index_in_dim(order, rank, 0, keepdims=False)
    ids = jnp.arange(8, dtype=jnp.int32)
    inverse = jnp.sum(jnp.where(order[None, :] == ids[:, None], ids[None, :], 0), axis=1)
    sc = jnp.concatenate(
        [jnp.stack([y, core, my_pair, rank]).astype(jnp.int32), inverse.astype(jnp.int32)]
    )

    offsets = jnp.arange(256, dtype=jnp.int32)
    pos = jnp.where(
        offsets < 128, my_pair * 128 + offsets, (15 - my_pair) * 128 + offsets - 128
    )
    freq = jnp.power(THETA, -2.0 * (jnp.arange(128) % 32).astype(F32) / HD)
    angle = pos.astype(F32)[:, None] * freq
    tables = (jnp.cos(angle), jnp.sin(angle))

    gain_rows = jnp.pad(
        jnp.stack([norm_first[0], norm_second[0], norm_first[1], norm_second[1]]),
        ((0, 12), (0, HALF - 144)),
    )
    own_c, own_m = [], []
    for layer in range(LAYERS):
        cols = []
        for g in range(KVH):
            cols += [w_key[layer][:, 64 * g : 64 * g + 64], w_value[layer][:, 64 * g : 64 * g + 64]]
        full = jnp.concatenate(cols + [w_query[layer], w_out[layer]], axis=1)
        own_c.append(
            jnp.concatenate(
                [halves_of(full), jnp.broadcast_to(gain_rows, (2, 16, HALF))], axis=1
            )
        )
        down = jnp.pad(w_down[layer].reshape(2, 192, D), ((0, 0), (0, 0), (0, HALF - D)))
        own_m.append(
            jnp.concatenate([halves_of(w_gate[layer]), halves_of(w_up[layer]), down], axis=1)
        )
    mine_c, mine_m = of_core(own_c[0], core), of_core(own_m[1], core)
    own_b = jnp.concatenate([own_c[1], own_m[0]], axis=1)
    mine_b = of_core(own_b, core)
    near_c = near(mine_c, (1, 2, 3))
    far_c = swap_all(near_c)
    gains = jnp.stack([mine_c[144:148, :144]] + [part[144:148, :144] for part in near_c])
    gains = jnp.roll(gains, y, axis=0).transpose(1, 0, 2).reshape(4, 1, D).astype(F32)
    gain_one, gain_two = (gains[0], gains[2]), (gains[1], gains[3])
    c_zero = ((own_c[0], *near_c, *far_c), 0)

    x = tokens[0].astype(F32)
    kv, q, normed = project(sc, x, gain_one[0], tables, c_zero)
    kv, mine_b = phase(kv, mine_b)
    b1, b3 = near(mine_b, (1, 3))
    kvs = all_pairs(kv, ("x", "core")).reshape(16, 128, 384)
    kvs, b1, b3, mine_b = phase(kvs, b1, b3, mine_b)
    (b2,) = near(mine_b, (2,))
    f1, f3 = swap_all((b1, b3))
    rows_out, log_total = attend(sc, q, kvs)
    rows_out, b2, f1, f3 = phase(rows_out, b2, f1, f3)
    f2 = swap_core(b2)
    rows_out, f2, mine_m = phase(rows_out, f2, mine_m)
    b_pieces = (own_b, b1, b2, b3, f1, f2, f3)
    c_one, m_zero = (b_pieces, 0), (b_pieces, CROWS)
    m1, m3 = near(mine_m, (1, 3))
    middle, normed_two, gate, up, after = feed(sc, x, rows_out, gain_two[0], c_zero, m_zero)
    saved = [(x, kvs, q, normed, rows_out, log_total, middle, normed_two, gate, up)]

    x = after
    kv, q, normed = project(sc, x, gain_one[1], tables, c_one)
    kv, m1, m3, mine_m = phase(kv, m1, m3, mine_m)
    (m2,) = near(mine_m, (2,))
    f1, f3 = swap_all((m1, m3))
    kvs = all_pairs(kv, ("x", "core")).reshape(16, 128, 384)
    kvs, m2, f1, f3 = phase(kvs, m2, f1, f3)
    f2 = swap_core(m2)
    rows_out, log_total = attend(sc, q, kvs)
    rows_out, f2 = phase(rows_out, f2)
    m_one = ((own_m[1], m1, m2, m3, f1, f2, f3), 0)
    middle, normed_two, gate, up, after = feed(sc, x, rows_out, gain_two[1], c_one, m_one)
    mixed = after.astype(BF)[None]

    upstream = cotangent[0].astype(F32)
    grad_middle, grad_attn, grad_rows, grad_gate, grad_up, hidden, grad_gain_two = feed_back(
        sc, upstream, middle, gate, up, gain_two[1], c_one, m_one
    )
    grad_q, grad_kvs = attend_back(sc, q, rows_out, grad_rows, log_total, tables, kvs)
    grad_kvs = all_pairs(grad_kvs.reshape(8, 2, 128, 384), ("x", "core"))
    keep_m, send_m = feed_grads(sc, normed_two, grad_gate, grad_up, hidden, upstream)
    grad_kvs, send_m = phase(grad_kvs, send_m)
    got_m = swap_core(send_m)
    upstream, keep_c, send_c = project_back(
        sc, x, gain_one[1], tables, grad_middle, grad_q, normed, rows_out, grad_attn,
        grad_gain_two, grad_kvs, c_one,
    )
    last = joined([(keep_m, got_m)])
    upstream, send_c, *last = phase(upstream, send_c, *last)
    got_c = swap_core(send_c)
    l1, l3 = sent(last, (1, 3))

    x, kvs, q, normed, rows_out, log_total, middle, normed_two, gate, up = saved[0]
    grad_middle, grad_attn, grad_rows, grad_gate, grad_up, hidden, grad_gain_two = feed_back(
        sc, upstream, middle, gate, up, gain_two[0], c_zero, m_zero
    )
    keep_m, send_m = feed_grads(sc, normed_two, grad_gate, grad_up, hidden, upstream)
    grad_rows, send_m, got_c, l1, l3, *last = phase(grad_rows, send_m, got_c, l1, l3, *last)
    (l2,) = sent(last, (2,))
    got_m = swap_core(send_m)
    grad_q, grad_kvs = attend_back(sc, q, rows_out, grad_rows, log_total, tables, kvs)
    first = joined([(keep_c, got_c), (keep_m, got_m)])
    last = quarters(added([last[0], l1, l2, l3]))
    grad_kvs, last, *first = phase(grad_kvs, last, *first)
    f1, f3 = sent(first, (1, 3))
    grad_kvs = all_pairs(grad_kvs.reshape(8, 2, 128, 384), ("x", "core"))
    keep_e, send_e = early_grads(sc, normed, grad_q, rows_out, grad_attn)
    early = joined([(keep_e, swap_core(send_e))])
    grad_kvs, last, f1, f3, *rest = phase(grad_kvs, last, f1, f3, *first, *early)
    first, early = rest[:4], rest[4:]
    last = all_pairs(last, "dp")
    (f2,) = sent(first, (2,))
    grad_tokens, keep, send = late_back(
        sc, x, gain_one[0], tables, grad_middle, grad_q, normed, grad_gain_two, grad_kvs, c_zero
    )
    last = summed_rows(last, 4)
    keep, send, last, *early = phase(keep, send, last, *early)
    late = added([keep, swap_core(send)]).astype(BF)
    e1, e2, e3 = sent(early, (1, 2, 3))
    late, last, f2 = phase(late, last, f2)
    late = summed_rows(all_pairs(late, "fsdp"), 4)
    last = around(last, "x").astype(BF)
    late, last, first = phase(late, last, quarters(added([first[0], f1, f2, f3])))
    first = all_pairs(first, "dp")
    late = around(late, "dp").astype(BF)
    early = around(added([early[0], e1, e2, e3]), "dp").astype(BF)
    late, early, first = phase(late, early, summed_rows(first, 4))
    late = around(late, "x").astype(BF)
    first = around(first, "x").astype(BF)
    last = all_pairs(copied(last, 4), "dp").reshape(MROWS, HALF)
    late, first, last = phase(late, first, last)
    early = around(early, "x").astype(BF)
    first = all_pairs(copied(first, 4), "dp").reshape(CROWS + MROWS, HALF)
    last = (last, swap_core(last))
    early = (early, swap_core(early))

    late = (late, swap_core(late))
    first = (first, swap_core(first))
    placed = assemble(assemble_last_kernel, (sc, *last), (), PLACED[:3])
    placed = assemble(assemble_first_kernel, (sc, *first), placed, PLACED)
    placed = assemble(assemble_rest_kernel, (sc, *early, *late), placed[3:], PLACED[3:], placed[:3])
    gate, up, down, query, out, key, value, gain_a, gain_b = placed
    return (
        mixed, grad_tokens[None], gain_a[:, 0, :144], query, key, value, out, gain_b[:, 0, :144],
        gate, up, down,
    )


def solution(mesh):
    split = jax.sharding.Mesh(mesh.devices.reshape(4, 4, 2, 4), ("dp", "x", "core", "fsdp"))
    rows = P(("dp", "fsdp"), ("x", "core"), None)
    flat, deep = P(None, "fsdp"), P(None, "fsdp", None)
    return jax.shard_map(
        local,
        mesh=split,
        in_specs=(rows, P(("dp", "fsdp"), None), rows, flat) + (deep,) * 4 + (flat,) + (deep,) * 3,
        out_specs=(rows, rows, flat) + (deep,) * 4 + (flat,) + (deep,) * 3,
        check_vma=False,
    )
```

```python
import jax
import jax.numpy as jnp
from jax import lax
from jax.experimental import pallas as pl
from jax.experimental.pallas import tpu as pltpu
from jax.sharding import PartitionSpec as P

NH = 9
KVH = 3
HD = 64
LAYERS = 2
D = 576
FF = 1536
HALF = 768
EPS = 1e-05
THETA = 100000.0
NEG = -1e30
BF = jnp.bfloat16
F32 = jnp.float32
CROWS = 160
MROWS = 480
VMEM_LIMIT = 60 * 1024 * 1024

ANY = pl.BlockSpec(memory_space=pl.ANY)
VM = pl.BlockSpec(memory_space=pltpu.VMEM)
SM = pl.BlockSpec(memory_space=pltpu.SMEM)


def nt(a, b):
    return lax.dot_general(a, b, (((1,), (1,)), ((), ())), preferred_element_type=F32)


def nn(a, b):
    return jnp.dot(a, b, preferred_element_type=F32)


def shaped(shape, dtype):
    return jax.ShapeDtypeStruct(shape, dtype)


def call(kernel, ins, specs, outs, scratch, flops, nbytes, far=0):
    return pl.pallas_call(
        kernel,
        out_shape=outs,
        in_specs=specs,
        out_specs=[VM] * (len(outs) - far) + [ANY] * far,
        scratch_shapes=scratch,
        compiler_params=pltpu.CompilerParams(vmem_limit_bytes=VMEM_LIMIT),
        cost_estimate=pl.CostEstimate(flops=1000, bytes_accessed=1000, transcendentals=0),
    )(*ins)


PIECES = 7


def unit_copies(sc, pieces, row, rows, dst, stride, split_rows, sems, first):
    core = sc[1]
    copies = []

    def add(src, slot, half):
        if split_rows:
            at = pl.multiple_of(slot * stride + half * (stride // 2), 16)
            target = dst.at[pl.ds(at, rows)]
        else:
            lanes = pl.ds(pl.multiple_of(half * HALF, 128), HALF)
            target = dst.at[pl.ds(pl.multiple_of(slot * stride, 16), rows), lanes]
        copies.append(pltpu.make_async_copy(src, target, sems.at[first + len(copies)]))

    for half in range(2):
        add(pieces[0].at[half, pl.ds(row, rows)], sc[0], half)
    for k in range(3):
        slot = lax.rem(sc[0] + k + 1, 4)
        add(pieces[1 + k].at[pl.ds(row, rows)], slot, core)
        add(pieces[4 + k].at[pl.ds(row, rows)], slot, 1 - core)
    for copy in copies:
        copy.start()
    return copies


def wait_all(copies):
    for copy in copies:
        copy.wait()


def lane_low(shape):
    return lax.rem(lax.broadcasted_iota(jnp.int32, shape, 1), 64) < 32


def rope(values, cosine, sine):
    width = values.shape[1]
    up = pltpu.roll(values, width - 32, 1)
    down = pltpu.roll(values, 32, 1)
    return values * cosine + jnp.where(lane_low(values.shape), -up, down) * sine


def rope_back(values, cosine, sine):
    width = values.shape[1]
    spun = values * sine
    up = pltpu.roll(spun, width - 32, 1)
    down = pltpu.roll(spun, 32, 1)
    return values * cosine + jnp.where(lane_low(values.shape), up, -down)


def table_lanes(narrow, kv_fill):
    first = lax.broadcasted_iota(jnp.int32, narrow.shape, 1) < HD
    pair = jnp.where(first, narrow, kv_fill)
    return jnp.concatenate([pair] * 3 + [narrow] * 4 + [jnp.where(first, narrow, 0.0)], axis=1)


def norm_factor(rows):
    return lax.rsqrt(jnp.mean(rows * rows, axis=-1, keepdims=True) + EPS)


def norm_back(rows, gain, upstream):
    factor = norm_factor(rows)
    scaled = upstream * gain
    inner = jnp.mean(scaled * rows, axis=-1, keepdims=True)
    grad_in = factor * scaled - rows * (factor * factor * factor) * inner
    return grad_in, jnp.sum(upstream * rows * factor, axis=0, keepdims=True)


def project_kernel(at, sc, x, gain, cosine, sine, *refs):
    pieces, (kv, q, normed_out, weight, sems) = refs[:PIECES], refs[PIECES:]
    copies = unit_copies(sc, pieces, at, 144, weight, 144, False, sems, 0)
    rows = x[...]
    normed = (rows * norm_factor(rows) * gain[...]).astype(BF)
    normed_out[...] = normed
    wait_all(copies)
    raw = nn(normed, weight[:, :1024])
    turned = rope(raw, table_lanes(cosine[...], 1.0), table_lanes(sine[...], 0.0))
    for s in range(8):
        kv[s, 0] = turned[:128, :384].astype(BF)
        kv[s, 1] = turned[128:, :384].astype(BF)
    q[...] = (turned[:, 384:960] * (HD**-0.5)).astype(BF)


def project(sc, x, gain, tables, pieces):
    pieces, at = pieces

    def kernel(*refs):
        project_kernel(at, *refs)

    return call(
        kernel,
        (sc, x, gain, *tables, *pieces),
        [SM] + [VM] * 4 + [ANY] * PIECES,
        (shaped((8, 2, 128, 384), BF), shaped((256, D), BF), shaped((256, D), BF)),
        [pltpu.VMEM((D, FF), BF), pltpu.SemaphoreType.DMA((8,))],
        2 * 256 * D * 960,
        5_000_000,
    )


def fill_padded(target, rows, first_row, first_lane):
    for g in range(KVH):
        for b in range(2):
            for h in range(3):
                head = 3 * g + h
                piece = rows[128 * b : 128 * b + 128, 64 * head : 64 * head + 64]
                zero = jnp.zeros_like(piece)
                pair = (piece, zero) if first_lane == 0 else (zero, piece)
                target[2 * g + b, first_row + 128 * h : first_row + 128 * h + 128] = (
                    jnp.concatenate(pair, axis=1).astype(BF)
                )


def slot_of(sc, i):
    pair = sc[2]
    is_low = i <= pair
    rank = jnp.where(is_low, sc[4 + min(i, 7)], sc[4 + lax.rem(8 - i + pair + 8, 8)])
    return is_low, 2 * rank + jnp.where(is_low, 0, 1)


def slots_of(sc):
    slots = []
    for i in range(9):
        is_low, block = slot_of(sc, i)
        slots.append((is_low, block, jnp.where(jnp.logical_or(i == sc[2], i == 8), 1.0, 0.0)))
    return slots + [(False, 2 * sc[4 + j], None) for j in range(8)]


def fill_mask(mask):
    key_at = lax.broadcasted_iota(jnp.int32, (128, 384), 0)
    query_at = lax.rem(lax.broadcasted_iota(jnp.int32, (128, 384), 1), 128)
    mask[...] = jnp.where(key_at <= query_at, 0.0, NEG)


def pick(is_low, low, high):
    if is_low is False:
        return high
    return jnp.where(is_low, low, high)


def add_to(is_low, low, high, value, combine):
    if is_low is False:
        return low, combine(high, value)
    return jnp.where(is_low, combine(low, value), low), jnp.where(is_low, high, combine(high, value))


def fill_turned(target, source, first_row):
    for at in range(6):
        target[at] = source[at, first_row : first_row + 384].astype(F32).T.astype(BF)


def attend_kernel(sc, q, held, out, log_total, padded, turned_q, scores, mask, heads):
    fill_padded(padded, q[...].astype(F32), 0, 0)
    fill_turned(turned_q, padded, 0)
    fill_mask(mask)
    slots = slots_of(sc)

    def key_head(g, carry):
        lanes = pl.ds(pl.multiple_of(128 * g, 128), 128)
        top_low = top_high = jnp.full((1, 384), NEG, F32)
        for k, (is_low, block, masked) in enumerate(slots):
            score = nn(held[block, :, lanes], turned_q[2 * g + pick(is_low, 0, 1)])
            if masked is not None:
                score = score + mask[...] * masked
            scores[k] = score
            top = jnp.max(score, axis=0, keepdims=True)
            top_low, top_high = add_to(is_low, top_low, top_high, top, jnp.maximum)
        total_low = total_high = jnp.zeros((1, 384), F32)
        rows_low = rows_high = jnp.zeros((HD, 384), F32)
        for k, (is_low, block, _) in enumerate(slots):
            expo = jnp.exp(scores[k] - pick(is_low, top_low, top_high))
            total = jnp.sum(expo, axis=0, keepdims=True)
            values = held[block, :, lanes].astype(F32).T[HD:].astype(BF)
            rows = nn(values, expo.astype(BF))
            total_low, total_high = add_to(is_low, total_low, total_high, total, jnp.add)
            rows_low, rows_high = add_to(is_low, rows_low, rows_high, rows, jnp.add)
        log_total[2 * g] = jnp.broadcast_to(top_low + jnp.log(total_low), (8, 384))
        log_total[2 * g + 1] = jnp.broadcast_to(top_high + jnp.log(total_high), (8, 384))
        heads[2 * g] = rows_low / total_low
        heads[2 * g + 1] = rows_high / total_high
        return carry

    lax.fori_loop(0, KVH, key_head, 0)
    for g in range(KVH):
        for b in range(2):
            turned = heads[2 * g + b].T.astype(BF)
            for h in range(3):
                head = 3 * g + h
                out[128 * b : 128 * b + 128, 64 * head : 64 * head + 64] = turned[
                    128 * h : 128 * h + 128
                ]


def attend(sc, q, kvs):
    return call(
        attend_kernel,
        (sc, q, kvs),
        [SM, VM, VM],
        (shaped((256, D), BF), shaped((6, 8, 384), F32)),
        [
            pltpu.VMEM((6, 384, 128), BF),
            pltpu.VMEM((6, 128, 384), BF),
            pltpu.VMEM((17, 128, 384), F32),
            pltpu.VMEM((128, 384), F32),
            pltpu.VMEM((6, HD, 384), F32),
        ],
        4 * 17 * 3 * 128 * 128 * 384,
        4_000_000,
    )


def attend_back_kernel(
    sc, q, rows_out, grad_out, log_total, cosine, sine, held, grad_q, grad_kv, both, delta, acc,
    early, slotted, dq, mask, probs, probs_low, grads_low, turned, turned_q, turned_g,
):
    fill_padded(both, q[...].astype(F32), 0, 0)
    fill_padded(both, grad_out[...].astype(F32), 384, 64)
    fill_turned(turned_q, both, 0)
    fill_turned(turned_g, both, 384)
    fill_mask(mask)
    product = rows_out[...].astype(F32) * grad_out[...].astype(F32)
    for g in range(KVH):
        for b in range(2):
            for h in range(3):
                head = 3 * g + h
                piece = product[128 * b : 128 * b + 128, 64 * head : 64 * head + 64]
                delta[2 * g + b, 0:1, 128 * h : 128 * h + 128] = jnp.sum(
                    piece.T, axis=0, keepdims=True
                )
    slots = slots_of(sc)

    def key_head(g, carry):
        lanes = pl.ds(pl.multiple_of(128 * g, 128), 128)
        for k, (is_low, block, masked) in enumerate(slots):
            at = 2 * g + pick(is_low, 0, 1)
            score = nn(held[block, :, lanes], turned_q[at])
            if masked is not None:
                score = score + mask[...] * masked
            prob = jnp.exp(score - log_total[at, 0:1])
            probs[k] = prob
            probs_low[k] = prob.astype(BF)
        for k, (is_low, block, _) in enumerate(slots):
            at = 2 * g + pick(is_low, 0, 1)
            tile = held[block, :, lanes]
            grad_prob = nn(tile, turned_g[at])
            grads_low[128 * k : 128 * k + 128] = (
                probs[k] * (grad_prob - delta[at, 0:1])
            ).astype(BF)
            turned[:, 128 * k : 128 * k + 128] = tile.astype(F32).T[:HD].astype(BF)
        low = jnp.zeros((HD, 384), F32)
        high = nn(turned[:, 1152:], grads_low[1152:])
        for k, (is_low, _, _) in enumerate(slots):
            at = 2 * g + pick(is_low, 0, 1)
            rows = slice(128 * k, 128 * k + 128)
            grad_score = grads_low[rows]
            if k < 9:
                low, high = add_to(is_low, low, high, nn(turned[:, rows], grad_score), jnp.add)
            pair = nn(grad_score, both[at, :384]) + nn(probs_low[k], both[at, 384:])
            if k < 9:
                slotted[k, :, lanes] = pair
            else:
                early[k - 9, :, lanes] = pair + jnp.where(
                    k - 9 <= sc[2], slotted[k - 9, :, lanes], 0.0
                )
        acc[2 * g] = low
        acc[2 * g + 1] = high
        return carry

    lax.fori_loop(0, KVH, key_head, 0)
    dq[...] = jnp.zeros_like(dq)
    for g in range(KVH):
        for b in range(2):
            heads = acc[2 * g + b].T
            for h in range(3):
                head = 3 * g + h
                dq[128 * b : 128 * b + 128, 64 * head : 64 * head + 64] = heads[
                    128 * h : 128 * h + 128
                ] * (HD**-0.5)
    turned = rope_back(
        dq[...], table_lanes(cosine[...], 1.0)[:, 384:], table_lanes(sine[...], 0.0)[:, 384:]
    )
    grad_q[...] = turned[:, :D].astype(BF)
    for r in range(8):
        pair = sc[13 + r]
        slot = 8 + sc[2] - pair
        grad_kv[2 * r] = early[pair].astype(BF)
        grad_kv[2 * r + 1] = jnp.where(
            slot <= 8, slotted[jnp.minimum(slot, 8)], 0.0
        ).astype(BF)


def attend_back(sc, q, rows_out, grad_out, log_total, tables, kvs):
    return call(
        attend_back_kernel,
        (sc, q, rows_out, grad_out, log_total, *tables, kvs),
        [SM] + [VM] * 7,
        (shaped((256, D), BF), shaped((16, 128, 384), BF)),
        [
            pltpu.VMEM((6, 768, 128), BF),
            pltpu.VMEM((6, 8, 384), F32),
            pltpu.VMEM((6, 64, 384), F32),
            pltpu.VMEM((8, 128, 384), F32),
            pltpu.VMEM((9, 128, 384), F32),
            pltpu.VMEM((256, 640), F32),
            pltpu.VMEM((128, 384), F32),
            pltpu.VMEM((17, 128, 384), F32),
            pltpu.VMEM((17, 128, 384), BF),
            pltpu.VMEM((17 * 128, 384), BF),
            pltpu.VMEM((HD, 17 * 128), BF),
            pltpu.VMEM((6, 128, 384), BF),
            pltpu.VMEM((6, 128, 384), BF),
        ],
        10 * 17 * 3 * 128 * 128 * 384,
        8_000_000,
    )


CHUNK = 512


def feed_kernel(sc, x, rows_out, gain, at_c, at_m, *refs):
    c_pieces, m_pieces, refs = refs[:PIECES], refs[PIECES : 2 * PIECES], refs[2 * PIECES :]
    middle_out, normed_out, gate_out, up_out, after = refs[:5]
    weight, gate_w, up_w, down_w, sems = refs[5:]
    first = unit_copies(sc, c_pieces, at_c, 144, weight, 144, False, sems, 0)
    second = unit_copies(sc, m_pieces, at_m, 144, gate_w, 144, False, sems, 8)
    second += unit_copies(sc, m_pieces, at_m + 144, 144, up_w, 144, False, sems, 16)
    third = unit_copies(sc, m_pieces, at_m + 288, 192, down_w, 384, True, sems, 24)
    wait_all(first)
    middle = x[...] + nn(rows_out[...], weight[:, 960:])
    middle_out[...] = middle
    normed = (middle * norm_factor(middle) * gain[...]).astype(BF)
    normed_out[...] = normed
    wait_all(second)
    wait_all(third)
    total = middle
    for at in range(0, FF, CHUNK):
        gate = nn(normed, gate_w[:, at : at + CHUNK])
        up = nn(normed, up_w[:, at : at + CHUNK])
        gate_out[:, at : at + CHUNK] = gate
        up_out[:, at : at + CHUNK] = up
        hidden = (gate * jax.nn.sigmoid(gate) * up).astype(BF)
        total = total + nn(hidden, down_w[at : at + CHUNK, :D])
    after[...] = total


def feed(sc, x, rows_out, gain, c_pieces, m_pieces):
    (c_pieces, at_c), (m_pieces, at_m) = c_pieces, m_pieces

    def kernel(sc, x, rows_out, gain, *refs):
        return feed_kernel(sc, x, rows_out, gain, at_c, at_m, *refs)

    wide = shaped((256, FF), F32)
    narrow = shaped((256, D), F32)
    return call(
        kernel,
        (sc, x, rows_out, gain, *c_pieces, *m_pieces),
        [SM] + [VM] * 3 + [ANY] * 2 * PIECES,
        (narrow, shaped((256, D), BF), wide, wide, narrow),
        [
            pltpu.VMEM((D, FF), BF),
            pltpu.VMEM((D, FF), BF),
            pltpu.VMEM((D, FF), BF),
            pltpu.VMEM((FF, HALF), BF),
            pltpu.SemaphoreType.DMA((32,)),
        ],
        2 * 256 * D * (D + 3 * FF),
        14_000_000,
    )


def feed_back_kernel(sc, upstream, middle, gate, up, gain, at_c, at_m, *refs):
    c_pieces, m_pieces, refs = refs[:PIECES], refs[PIECES : 2 * PIECES], refs[2 * PIECES :]
    grad_middle, grad_attn_out, grad_rows, grad_gate_out, grad_up_out, hidden_out, grad_gain = refs[
        :7
    ]
    weight, gate_w, up_w, down_w, sems = refs[7:]
    third = unit_copies(sc, m_pieces, at_m + 288, 192, down_w, 384, True, sems, 24)
    second = unit_copies(sc, m_pieces, at_m, 144, gate_w, 144, False, sems, 8)
    second += unit_copies(sc, m_pieces, at_m + 144, 144, up_w, 144, False, sems, 16)
    first = unit_copies(sc, c_pieces, at_c, 144, weight, 144, False, sems, 0)
    grad_down = upstream[...].astype(BF)
    wait_all(third)
    wait_all(second)
    grad_normed = jnp.zeros((256, D), F32)
    for at in range(0, FF, CHUNK):
        lanes = slice(at, at + CHUNK)
        grad_hidden = nt(grad_down, down_w[at : at + CHUNK, :D])
        gate_act, up_proj = gate[:, lanes], up[:, lanes]
        sigma = jax.nn.sigmoid(gate_act)
        silu = gate_act * sigma
        grad_gate = (grad_hidden * up_proj * sigma * (1.0 + gate_act * (1.0 - sigma))).astype(BF)
        grad_up = (grad_hidden * silu).astype(BF)
        grad_gate_out[:, lanes] = grad_gate
        grad_up_out[:, lanes] = grad_up
        hidden_out[:, lanes] = (silu * up_proj).astype(BF)
        grad_normed = grad_normed + nt(grad_gate, gate_w[:, lanes]) + nt(grad_up, up_w[:, lanes])
    back, grad_gain_sum = norm_back(middle[...], gain[...], grad_normed)
    grad_gain[...] = grad_gain_sum
    total = upstream[...] + back
    grad_middle[...] = total
    grad_attn = total.astype(BF)
    grad_attn_out[...] = grad_attn
    wait_all(first)
    grad_rows[...] = nt(grad_attn, weight[:, 960:]).astype(BF)


def feed_back(sc, upstream, middle, gate, up, gain, c_pieces, m_pieces):
    (c_pieces, at_c), (m_pieces, at_m) = c_pieces, m_pieces

    def kernel(sc, upstream, middle, gate, up, gain, *refs):
        return feed_back_kernel(sc, upstream, middle, gate, up, gain, at_c, at_m, *refs)

    wide = shaped((256, FF), BF)
    return call(
        kernel,
        (sc, upstream, middle, gate, up, gain, *c_pieces, *m_pieces),
        [SM] + [VM] * 5 + [ANY] * 2 * PIECES,
        (
            shaped((256, D), F32),
            shaped((256, D), BF),
            shaped((256, D), BF),
            wide,
            wide,
            wide,
            shaped((1, D), F32),
        ),
        [
            pltpu.VMEM((D, FF), BF),
            pltpu.VMEM((D, FF), BF),
            pltpu.VMEM((D, FF), BF),
            pltpu.VMEM((FF, HALF), BF),
            pltpu.SemaphoreType.DMA((32,)),
        ],
        2 * 256 * D * (D + 3 * FF),
        14_000_000,
    )


def store_piece(sc, parts, owner, half, rows, value, own_first=True):
    slot = lax.rem(owner - sc[0] + 4, 4) if own_first else owner
    parts[jnp.where(sc[1] == half, 0, 1), slot, rows] = value


def send_parts(parts, keep, send, sems):
    copies = [
        pltpu.make_async_copy(parts.at[k], ref, sems.at[k]) for k, ref in enumerate((keep, send))
    ]
    for copy in copies:
        copy.start()
    wait_all(copies)


def parts_scratch(rows):
    return [pltpu.VMEM((2, 4, rows, HALF), BF), pltpu.SemaphoreType.DMA((2,))]


def feed_grads_kernel(sc, normed, grad_gate, grad_up, hidden, upstream, keep, send, turned, tall, *held):
    turned[...] = normed[...].astype(F32).T.astype(BF)
    for at in range(0, FF, CHUNK):
        tall[at : at + CHUNK] = hidden[:, at : at + CHUNK].astype(F32).T.astype(BF)
    grad_down = jnp.concatenate(
        [upstream[...], jnp.zeros((256, HALF - D), F32)], axis=1
    ).astype(BF)
    for half in range(2):
        lanes = slice(HALF * half, HALF * half + HALF)
        for owner in range(4):
            left = turned[144 * owner : 144 * owner + 144]
            at = 384 * owner + 192 * half
            for rows, value in (
                (slice(0, 144), nn(left, grad_gate[:, lanes])),
                (slice(144, 288), nn(left, grad_up[:, lanes])),
                (slice(288, 480), nn(tall[at : at + 192], grad_down)),
            ):
                store_piece(sc, held[0], owner, half, rows, value.astype(BF))
    send_parts(held[0], keep, send, held[1])


def feed_grads(sc, normed, grad_gate, grad_up, hidden, upstream):
    out = shaped((4, MROWS, HALF), BF)
    return call(
        feed_grads_kernel,
        (sc, normed, grad_gate, grad_up, hidden, upstream),
        [SM] + [VM] * 5,
        (out, out),
        [pltpu.VMEM((D, 256), BF), pltpu.VMEM((FF, 256), BF)] + parts_scratch(MROWS),
        2 * 256 * D * 3 * FF,
        9_000_000,
        2,
    )


def grad_kv_rows(grad_kvs, cosine, sine, half):
    total = grad_kvs[0, half].astype(F32)
    for r in range(1, 8):
        total = total + grad_kvs[r, half].astype(F32)
    rows = slice(128 * half, 128 * half + 128)
    cos_t, sin_t = table_lanes(cosine[rows], 1.0), table_lanes(sine[rows], 0.0)
    return rope_back(total, cos_t[:, :384], sin_t[:, :384])


def project_back_kernel(
    at, sc, x, gain, cosine, sine, grad_middle, grad_q, normed, attn_rows, grad_attn, gain_two,
    grad_kvs, *refs,
):
    pieces, (upstream, keep, send, weight, buf, turned, sems, *held) = (
        refs[:PIECES], refs[PIECES:]
    )
    copies = unit_copies(sc, pieces, at, 144, weight, 144, False, sems, 0)
    for half in range(2):
        rows = slice(128 * half, 128 * half + 128)
        buf[rows, :384] = grad_kv_rows(grad_kvs, cosine, sine, half)
    buf[:, 384:960] = grad_q[...].astype(F32)
    buf[:, 960:] = grad_attn[...].astype(F32)
    inner = buf[:, :960].astype(BF)
    wait_all(copies)
    grad_normed = nt(inner, weight[:, :960])
    back, grad_gain = norm_back(x[...], gain[...], grad_normed)
    upstream[...] = grad_middle[...] + back
    turned[0] = normed[...].astype(F32).T.astype(BF)
    turned[1] = attn_rows[...].astype(F32).T.astype(BF)
    right = [buf[:, :HALF].astype(BF), buf[:, HALF:].astype(BF)]
    lane = lax.broadcasted_iota(jnp.int32, (144, HALF), 1)
    gains = (grad_gain, gain_two[...])
    for owner in range(4):
        rows = slice(144 * owner, 144 * owner + 144)
        for half in range(2):
            value = nn(turned[0, rows], right[half])
            if half == 1:
                value = jnp.where(lane < 192, value, nn(turned[1, rows], right[1]))
            store_piece(sc, held[0], owner, half, slice(0, 144), value.astype(BF), False)
            row = jnp.concatenate([gains[half][:, rows], jnp.zeros((1, HALF - 144), F32)], axis=1)
            block = jnp.broadcast_to(row, (16, HALF))
            store_piece(sc, held[0], owner, half, slice(144, 160), block.astype(BF), False)
    send_parts(held[0], keep, send, held[1])


def project_back(
    sc, x, gain, tables, grad_middle, grad_q, normed, attn_rows, grad_attn, gain_two, grad_kvs, pieces
):
    out = shaped((4, CROWS, HALF), BF)
    pieces, at = pieces

    def kernel(*refs):
        project_back_kernel(at, *refs)

    return call(
        kernel,
        (
            sc, x, gain, *tables, grad_middle, grad_q, normed, attn_rows, grad_attn, gain_two,
            grad_kvs, *pieces,
        ),
        [SM] + [VM] * 11 + [ANY] * PIECES,
        (shaped((256, D), F32), out, out),
        [
            pltpu.VMEM((D, FF), BF),
            pltpu.VMEM((256, FF), F32),
            pltpu.VMEM((2, D, 256), BF),
            pltpu.SemaphoreType.DMA((8,)),
        ]
        + parts_scratch(CROWS),
        2 * 256 * D * (960 + FF),
        10_000_000,
        2,
    )


def early_grads_kernel(sc, normed, grad_q, attn_rows, grad_attn, keep, send, turned, *held):
    turned[0] = normed[...].astype(F32).T.astype(BF)
    turned[1] = attn_rows[...].astype(F32).T.astype(BF)
    for half, right in enumerate((grad_q, grad_attn)):
        for owner in range(4):
            value = nn(turned[half, 144 * owner : 144 * owner + 144], right[...])
            value = jnp.concatenate([value, jnp.zeros((144, HALF - D), F32)], axis=1)
            value = jnp.concatenate([value, jnp.zeros((16, HALF), F32)], axis=0)
            store_piece(sc, held[0], owner, half, slice(0, CROWS), value.astype(BF))
    send_parts(held[0], keep, send, held[1])


def early_grads(sc, normed, grad_q, attn_rows, grad_attn):
    out = shaped((4, CROWS, HALF), BF)
    return call(
        early_grads_kernel,
        (sc, normed, grad_q, attn_rows, grad_attn),
        [SM] + [VM] * 4,
        (out, out),
        [pltpu.VMEM((2, D, 256), BF)] + parts_scratch(CROWS),
        4 * 256 * D * D,
        4_000_000,
        2,
    )


LROWS = 80


def late_back_kernel(
    at, sc, x, gain, cosine, sine, grad_middle, grad_q, normed, gain_two, grad_kvs, *refs
):
    pieces, (grad_tokens, parts, weight, buf, turned, sems) = refs[:PIECES], refs[PIECES:]
    copies = unit_copies(sc, pieces, at, 144, weight, 144, False, sems, 0)
    for half in range(2):
        rows = slice(128 * half, 128 * half + 128)
        buf[rows, :384] = grad_kv_rows(grad_kvs, cosine, sine, half).astype(BF)
    buf[:, 384:] = grad_q[...]
    wait_all(copies)
    grad_normed = nt(buf[...], weight[:, :960])
    back, grad_gain = norm_back(x[...], gain[...], grad_normed)
    grad_tokens[...] = (grad_middle[...] + back).T.astype(BF)
    turned[...] = normed[...].astype(F32).T.astype(BF)
    gains = (grad_gain, gain_two[...])
    for owner in range(4):
        rows = slice(144 * owner, 144 * owner + 144)
        value = nn(turned[rows], buf[:, :384])
        for half in range(2):
            row = jnp.concatenate([gains[half][:, rows], jnp.zeros((1, 384 - 144), F32)], axis=1)
            block = jnp.broadcast_to(row, (8, 384))
            piece = jnp.concatenate([value[72 * half : 72 * half + 72], block], axis=0)
            parts[4 * half + owner] = piece.astype(BF)


def late_back(sc, x, gain, tables, grad_middle, grad_q, normed, gain_two, grad_kvs, pieces):
    pieces, at = pieces

    def kernel(*refs):
        late_back_kernel(at, *refs)

    return call(
        kernel,
        (sc, x, gain, *tables, grad_middle, grad_q, normed, gain_two, grad_kvs, *pieces),
        [SM] + [VM] * 9 + [ANY] * PIECES,
        (shaped((D, 256), BF), shaped((8, LROWS, 384), BF)),
        [
            pltpu.VMEM((D, FF), BF),
            pltpu.VMEM((256, 960), BF),
            pltpu.VMEM((D, 256), BF),
            pltpu.SemaphoreType.DMA((8,)),
        ],
        2 * 256 * D * (960 + 384),
        6_000_000,
    )


def halves_in_order(sc, mine, other):
    rows = mine[...].astype(F32), other[...].astype(F32)
    is_first = sc[1] == 0
    return jnp.where(is_first, rows[0], rows[1]), jnp.where(is_first, rows[1], rows[0])


def in_order(sc, mine, other, spread):
    first = MROWS // 4
    second = mine.shape[1] - first
    for k in range(4):
        slot = lax.rem(sc[12] + k, 4)
        at_first = pl.ds(pl.multiple_of(slot * first, 8), first)
        at_second = pl.ds(pl.multiple_of(MROWS + slot * second, 8), second)
        for side, ref in enumerate((mine, other)):
            spread[side, at_first] = ref[k, :first].astype(F32)
            spread[side, at_second] = ref[k, first:].astype(F32)
    return spread.at[sc[1]], spread.at[1 - sc[1]]


def heads_apart(rows):
    keys = [rows[:, 128 * g : 128 * g + HD] for g in range(KVH)]
    values = [rows[:, 128 * g + HD : 128 * g + 128] for g in range(KVH)]
    return jnp.concatenate(keys, axis=1), jnp.concatenate(values, axis=1)


def place_all(pairs, sems, layer):
    copies = [
        pltpu.make_async_copy(src, dst.at[layer], sems.at[k]) for k, (src, dst) in enumerate(pairs)
    ]
    for copy in copies:
        copy.start()
    return copies


def fill_wide(left, right, at, gate, up, down):
    for k, rows in enumerate((left, right)):
        lanes = slice(HALF * k, HALF * k + HALF)
        gate[:, lanes] = rows[at : at + 144]
        up[:, lanes] = rows[at + 144 : at + 288]
    halves = [rows[at + 288 : at + 480, :D] for rows in (left, right)]
    down[...] = jnp.concatenate(halves, axis=0).T


def fill_square(left, right, at, query, out, key, value):
    query[:, :384], query[:, 384:] = left[at : at + 144, 384:], right[at : at + 144, :192]
    out[...] = right[at : at + 144, 192:]
    key[...], value[...] = heads_apart(left[at : at + 144, :384])


def assemble_kernel(sc, mine, other, e_mine, e_other, l_mine, l_other, *refs):
    (gain_a, gain_b), outs, held, spread, sems = refs[:2], refs[2:9], refs[9:23], refs[23], refs[24]
    left, right = in_order(sc, mine, other, spread)
    fill_wide(left, right, 0, *held[:3])
    copies = place_all(zip(held[:3], outs[:3]), sems, 1)
    fill_wide(left, right, MROWS + CROWS, *held[3:6])
    copies += place_all(zip(held[3:6], outs[:3]), sems.at[pl.ds(3, 3)], 0)
    fill_square(left, right, MROWS, *held[6:10])
    copies += place_all(zip(held[6:10], outs[3:]), sems.at[pl.ds(6, 4)], 1)
    row = MROWS + 144
    gain_a[1:2], gain_b[1:2] = left[row : row + 1, :144], right[row : row + 1, :144]
    query, out, key, value = held[10:]
    left, right = halves_in_order(sc, e_mine, e_other)
    query[...], out[...] = left[:144, :D], right[:144, :D]
    left, right = halves_in_order(sc, l_mine, l_other)
    key[...], value[...] = heads_apart(jnp.concatenate([left[:72], right[:72]], axis=0))
    gain_a[0:1], gain_b[0:1] = left[72:73, :144], right[72:73, :144]
    copies += place_all(zip(held[10:], outs[3:]), sems.at[pl.ds(10, 4)], 0)
    wait_all(copies)


PLACED = ((144, FF),) * 2 + ((D, 384),) + ((144, D),) * 2 + ((144, KVH * HD),) * 2


def assemble(*ins):
    held = PLACED[:3] + PLACED[:3] + PLACED[3:] + PLACED[3:]
    return pl.pallas_call(
        assemble_kernel,
        out_shape=(shaped((LAYERS, 144), F32),) * 2
        + tuple(shaped((LAYERS,) + shape, F32) for shape in PLACED),
        in_specs=[SM] + [VM] * (len(ins) - 1),
        out_specs=[VM] * 2 + [ANY] * len(PLACED),
        scratch_shapes=[pltpu.VMEM(shape, F32) for shape in held]
        + [
            pltpu.VMEM((2, 4 * ins[1].shape[1], HALF), F32),
            pltpu.SemaphoreType.DMA((len(held),)),
        ],
        compiler_params=pltpu.CompilerParams(vmem_limit_bytes=VMEM_LIMIT),
        cost_estimate=pl.CostEstimate(flops=1000, bytes_accessed=1000, transcendentals=0),
    )(*ins)


def ring(axis, shift):
    n = lax.axis_size(axis)
    return [(i, (i + shift) % n) for i in range(n)]


def swap_core(value):
    return lax.ppermute(value, "core", [(0, 1), (1, 0)])


def all_pairs(value, axis):
    return lax.all_to_all(value, axis, 0, 0, tiled=True)


def copied(value, n):
    return jnp.broadcast_to(value[None], (n,) + value.shape)


def added(parts):
    total = parts[0].astype(F32)
    for part in parts[1:]:
        total = total + part.astype(F32)
    return total


def summed_rows(pieces, n):
    return added([pieces[k] for k in range(n)])


def around(own, axis):
    own = own.astype(BF)
    return added([own] + [lax.ppermute(own, axis, ring(axis, s)) for s in (1, 2, 3)])


def phase(*values):
    return lax.optimization_barrier(values)


def sent(pieces, shifts):
    return [lax.ppermute(pieces[k], "fsdp", ring("fsdp", k)) for k in shifts]


def near(mine, shifts):
    return [lax.ppermute(mine, "fsdp", ring("fsdp", -k)) for k in shifts]


def gathered(quarter):
    parts = [quarter] + [lax.ppermute(quarter, "dp", ring("dp", -k)) for k in (1, 2, 3)]
    return jnp.stack(parts)


def swap_all(parts):
    return [swap_core(part) for part in parts]


def joined(parts):
    return [
        jnp.concatenate([added([keep[k], got[k]]).astype(BF) for keep, got in parts], axis=0)
        for k in range(4)
    ]


def quarters(total):
    return total.astype(BF).reshape(4, -1, HALF)


def halves_of(full):
    return jnp.stack([full[:, :HALF], full[:, HALF:]])


def of_core(own, core):
    return lax.dynamic_index_in_dim(own, core, 0, keepdims=False)


def local(
    tokens, pair_order, cotangent, norm_first, w_query, w_key, w_value, w_out, norm_second,
    w_gate, w_up, w_down,
):
    core = lax.axis_index("core")
    rank = lax.axis_index("x") * 2 + core
    y = lax.axis_index("fsdp")
    order = pair_order[0]
    my_pair = lax.dynamic_index_in_dim(order, rank, 0, keepdims=False)
    ids = jnp.arange(8, dtype=jnp.int32)
    inverse = jnp.sum(jnp.where(order[None, :] == ids[:, None], ids[None, :], 0), axis=1)
    sc = jnp.concatenate(
        [
            jnp.stack([y, core, my_pair, rank]).astype(jnp.int32),
            inverse.astype(jnp.int32),
            lax.axis_index("dp").astype(jnp.int32)[None],
            order.astype(jnp.int32),
        ]
    )

    offsets = jnp.arange(256, dtype=jnp.int32)
    pos = jnp.where(
        offsets < 128, my_pair * 128 + offsets, (15 - my_pair) * 128 + offsets - 128
    )
    freq = jnp.power(THETA, -2.0 * (jnp.arange(128) % 32).astype(F32) / HD)
    angle = pos.astype(F32)[:, None] * freq
    tables = (jnp.cos(angle), jnp.sin(angle))

    gain_rows = jnp.pad(
        jnp.stack([norm_first[0], norm_second[0], norm_first[1], norm_second[1]]),
        ((0, 12), (0, HALF - 144)),
    )
    def c_slices(layer):
        cols = []
        for g in range(KVH):
            cols += [w_key[layer][:, 64 * g : 64 * g + 64], w_value[layer][:, 64 * g : 64 * g + 64]]
        full = jnp.concatenate(cols + [w_query[layer], w_out[layer]], axis=1)
        return jnp.concatenate(
            [halves_of(full), jnp.broadcast_to(gain_rows, (2, 16, HALF))], axis=1
        )

    def m_slices(gate, up, down):
        down = jnp.pad(down.reshape(2, 192, D), ((0, 0), (0, 0), (0, HALF - D)))
        return jnp.concatenate([halves_of(gate), halves_of(up), down], axis=1)

    own_c = c_slices(0)
    mine_c = of_core(own_c, core)
    own_b = m_slices(w_gate[0], w_up[0], w_down[0])
    mine_b = of_core(own_b, core)
    near_c = near(mine_c, (1, 2, 3))
    *near_c, mine_b, own_b = phase(*near_c, mine_b, own_b)
    far_c = swap_all(near_c)
    gains = jnp.stack([mine_c[144:148, :144]] + [part[144:148, :144] for part in near_c])
    gains = jnp.roll(gains, y, axis=0).transpose(1, 0, 2).reshape(4, 1, D).astype(F32)
    gain_one, gain_two = (gains[0], gains[2]), (gains[1], gains[3])
    c_zero = ((own_c, *near_c, *far_c), 0)

    x = tokens[0].astype(F32)
    b1, b3 = near(mine_b, (1, 3))
    kv, q, normed = project(sc, x, gain_one[0], tables, c_zero)
    kv, b1, b3, mine_b, *late_w = phase(kv, b1, b3, mine_b, w_gate[1], w_up[1], w_down[1])
    (b2,) = near(mine_b, (2,))
    f1, f3 = swap_all((b1, b3))
    kvs = all_pairs(kv, ("x", "core")).reshape(16, 128, 384)
    own_d, own_m = c_slices(1), m_slices(*late_w)
    mine_d, mine_m = of_core(own_d, core), of_core(own_m, core)
    kvs, b2, f1, f3, mine_d, own_d, mine_m, own_m = phase(
        kvs, b2, f1, f3, mine_d, own_d, mine_m, own_m
    )
    f2 = swap_core(b2)
    near_d = near(mine_d, (1, 2, 3))
    rows_out, log_total = attend(sc, q, kvs)
    rows_out, f2, mine_m, *near_d = phase(rows_out, f2, mine_m, *near_d)
    m_zero = ((own_b, b1, b2, b3, f1, f2, f3), 0)
    c_one = ((own_d, *near_d, *swap_all(near_d)), 0)
    m1, m3 = near(mine_m, (1, 3))
    middle, normed_two, gate, up, after = feed(sc, x, rows_out, gain_two[0], c_zero, m_zero)
    saved = [(x, kvs, q, normed, rows_out, log_total, middle, normed_two, gate, up)]

    x = after
    kv, q, normed = project(sc, x, gain_one[1], tables, c_one)
    kv, m1, m3, mine_m = phase(kv, m1, m3, mine_m)
    (m2,) = near(mine_m, (2,))
    f1, f3 = swap_all((m1, m3))
    kvs = all_pairs(kv, ("x", "core")).reshape(16, 128, 384)
    kvs, m2, f1, f3 = phase(kvs, m2, f1, f3)
    f2 = swap_core(m2)
    rows_out, log_total = attend(sc, q, kvs)
    m_one = ((own_m, m1, m2, m3, f1, f2, f3), 0)
    middle, normed_two, gate, up, after = feed(sc, x, rows_out, gain_two[1], c_one, m_one)
    mixed = after.astype(BF)[None]

    upstream = cotangent[0].astype(F32)
    grad_middle, grad_attn, grad_rows, grad_gate, grad_up, hidden, grad_gain_two = feed_back(
        sc, upstream, middle, gate, up, gain_two[1], c_one, m_one
    )
    keep_m, send_m = feed_grads(sc, normed_two, grad_gate, grad_up, hidden, upstream)
    grad_rows, send_m = phase(grad_rows, send_m)
    got_m = swap_core(send_m)
    grad_q, grad_kvs = attend_back(sc, q, rows_out, grad_rows, log_total, tables, kvs)
    last = joined([(keep_m, got_m)])
    grad_kvs, *last = phase(grad_kvs, *last)
    l1, l3 = sent(last, (1, 3))
    grad_kvs = all_pairs(grad_kvs.reshape(8, 2, 128, 384), ("x", "core"))
    grad_kvs, l1, l3, *last = phase(grad_kvs, l1, l3, *last)
    (l2,) = sent(last, (2,))
    upstream, keep_c, send_c = project_back(
        sc, x, gain_one[1], tables, grad_middle, grad_q, normed, rows_out, grad_attn,
        grad_gain_two, grad_kvs, c_one,
    )

    x, kvs, q, normed, rows_out, log_total, middle, normed_two, gate, up = saved[0]
    grad_middle, grad_attn, grad_rows, grad_gate, grad_up, hidden, grad_gain_two = feed_back(
        sc, upstream, middle, gate, up, gain_two[0], c_zero, m_zero
    )
    last = quarters(added([last[0], l1, l2, l3]))
    grad_gate, send_c, last = phase(grad_gate, send_c, last)
    last = all_pairs(last, "dp")
    got_c = swap_core(send_c)
    keep_m, send_m = feed_grads(sc, normed_two, grad_gate, grad_up, hidden, upstream)
    last = summed_rows(last, 4)
    grad_rows, send_m, last, got_c = phase(grad_rows, send_m, last, got_c)
    middle_c = all_pairs(added([keep_c, got_c]).astype(BF), "fsdp")
    got_m = swap_core(send_m)
    last = around(last, "x").astype(BF)
    grad_q, grad_kvs = attend_back(sc, q, rows_out, grad_rows, log_total, tables, kvs)
    first = joined([(keep_m, got_m)])
    grad_kvs, grad_q, last, middle_c, *first = phase(grad_kvs, grad_q, last, middle_c, *first)
    f1, f2, f3 = sent(first, (1, 2, 3))
    grad_kvs = all_pairs(grad_kvs.reshape(8, 2, 128, 384), ("x", "core"))
    keep_e, send_e = early_grads(sc, normed, grad_q, rows_out, grad_attn)
    early = joined([(keep_e, swap_core(send_e))])
    first = quarters(
        jnp.concatenate([summed_rows(middle_c, 4), added([first[0], f1, f2, f3])], axis=0)
    )
    grad_kvs, first, last, *early = phase(grad_kvs, first, last, *early)
    first = all_pairs(first, "dp")
    e1, e2, e3 = sent(early, (1, 2, 3))
    grad_tokens, late = late_back(
        sc, x, gain_one[0], tables, grad_middle, grad_q, normed, grad_gain_two, grad_kvs, c_zero
    )

    early = added([early[0], e1, e2, e3]).astype(BF)
    first = summed_rows(first, 4).astype(BF)
    late, first, early = phase(late, first, early)
    late = summed_rows(all_pairs(late, ("core", "fsdp")), 8).astype(BF)
    first = jnp.concatenate([last, around(first, "x").astype(BF)], axis=0)
    early = around(early, "dp").astype(BF)
    late, first, early = phase(late, first, early)
    late = summed_rows(all_pairs(copied(late, 16), ("dp", "x")), 16).astype(BF)
    first = gathered(first)
    early = around(early, "x").astype(BF)
    late, first, early = phase(late, first, early)
    gain_a, gain_b, gate, up, down, query, out, key, value = assemble(
        sc, first, swap_core(first), early, swap_core(early), late, swap_core(late)
    )
    return (
        mixed, grad_tokens.T[None], gain_a, query, key, value, out, gain_b, gate, up,
        down.transpose(0, 2, 1),
    )


def solution(mesh):
    split = jax.sharding.Mesh(mesh.devices.reshape(4, 4, 2, 4), ("dp", "x", "core", "fsdp"))
    rows = P(("dp", "fsdp"), ("x", "core"), None)
    flat, deep = P(None, "fsdp"), P(None, "fsdp", None)
    return jax.shard_map(
        local,
        mesh=split,
        in_specs=(rows, P(("dp", "fsdp"), None), rows, flat) + (deep,) * 4 + (flat,) + (deep,) * 3,
        out_specs=(rows, rows, flat) + (deep,) * 4 + (flat,) + (deep,) * 3,
        check_vma=False,
    )
```

```python
import jax
import jax.numpy as jnp
from jax import lax
from jax.experimental import pallas as pl
from jax.experimental.pallas import tpu as pltpu
from jax.sharding import PartitionSpec as P

NH = 9
KVH = 3
HD = 64
LAYERS = 2
D = 576
FF = 1536
HALF = 768
EPS = 1e-05
THETA = 100000.0
NEG = -1e30
BF = jnp.bfloat16
F32 = jnp.float32
CROWS = 160
MROWS = 480
VMEM_LIMIT = 60 * 1024 * 1024

ANY = pl.BlockSpec(memory_space=pl.ANY)
VM = pl.BlockSpec(memory_space=pltpu.VMEM)
SM = pl.BlockSpec(memory_space=pltpu.SMEM)


def nt(a, b):
    return lax.dot_general(a, b, (((1,), (1,)), ((), ())), preferred_element_type=F32)


def nn(a, b):
    return jnp.dot(a, b, preferred_element_type=F32)


def shaped(shape, dtype):
    return jax.ShapeDtypeStruct(shape, dtype)


def call(kernel, ins, specs, outs, scratch, flops, nbytes, far=0):
    return pl.pallas_call(
        kernel,
        out_shape=outs,
        in_specs=specs,
        out_specs=[VM] * (len(outs) - far) + [ANY] * far,
        scratch_shapes=scratch,
        compiler_params=pltpu.CompilerParams(vmem_limit_bytes=VMEM_LIMIT),
        cost_estimate=pl.CostEstimate(flops=1000, bytes_accessed=1000, transcendentals=0),
    )(*ins)


PIECES = 7


def unit_copies(sc, pieces, row, rows, dst, stride, split_rows, sems, first):
    core = sc[1]
    copies = []

    def add(src, slot, half):
        if split_rows:
            at = pl.multiple_of(slot * stride + half * (stride // 2), 16)
            target = dst.at[pl.ds(at, rows)]
        else:
            lanes = pl.ds(pl.multiple_of(half * HALF, 128), HALF)
            target = dst.at[pl.ds(pl.multiple_of(slot * stride, 16), rows), lanes]
        copies.append(pltpu.make_async_copy(src, target, sems.at[first + len(copies)]))

    for half in range(2):
        add(pieces[0].at[half, pl.ds(row, rows)], sc[0], half)
    for k in range(3):
        slot = lax.rem(sc[0] + k + 1, 4)
        add(pieces[1 + k].at[pl.ds(row, rows)], slot, core)
        add(pieces[4 + k].at[pl.ds(row, rows)], slot, 1 - core)
    for copy in copies:
        copy.start()
    return copies


def wait_all(copies):
    for copy in copies:
        copy.wait()


def lane_low(shape):
    return lax.rem(lax.broadcasted_iota(jnp.int32, shape, 1), 64) < 32


def rope(values, cosine, sine):
    width = values.shape[1]
    up = pltpu.roll(values, width - 32, 1)
    down = pltpu.roll(values, 32, 1)
    return values * cosine + jnp.where(lane_low(values.shape), -up, down) * sine


def rope_back(values, cosine, sine):
    width = values.shape[1]
    spun = values * sine
    up = pltpu.roll(spun, width - 32, 1)
    down = pltpu.roll(spun, 32, 1)
    return values * cosine + jnp.where(lane_low(values.shape), up, -down)


def table_lanes(narrow, kv_fill):
    first = lax.broadcasted_iota(jnp.int32, narrow.shape, 1) < HD
    pair = jnp.where(first, narrow, kv_fill)
    return jnp.concatenate([pair] * 3 + [narrow] * 4 + [jnp.where(first, narrow, 0.0)], axis=1)


def norm_factor(rows):
    return lax.rsqrt(jnp.mean(rows * rows, axis=-1, keepdims=True) + EPS)


def norm_back(rows, gain, upstream):
    factor = norm_factor(rows)
    scaled = upstream * gain
    inner = jnp.mean(scaled * rows, axis=-1, keepdims=True)
    grad_in = factor * scaled - rows * (factor * factor * factor) * inner
    return grad_in, jnp.sum(upstream * rows * factor, axis=0, keepdims=True)


def project_kernel(at, sc, x, gain, cosine, sine, *refs):
    pieces, (kv, q, normed_out, weight, sems) = refs[:PIECES], refs[PIECES:]
    copies = unit_copies(sc, pieces, at, 144, weight, 144, False, sems, 0)
    rows = x[...]
    normed = (rows * norm_factor(rows) * gain[...]).astype(BF)
    normed_out[...] = normed
    wait_all(copies)
    raw = nn(normed, weight[:, :1024])
    turned = rope(raw, table_lanes(cosine[...], 1.0), table_lanes(sine[...], 0.0))
    for s in range(8):
        kv[s, 0] = turned[:128, :384].astype(BF)
        kv[s, 1] = turned[128:, :384].astype(BF)
    q[...] = (turned[:, 384:960] * (HD**-0.5)).astype(BF)


def project(sc, x, gain, tables, pieces):
    pieces, at = pieces

    def kernel(*refs):
        project_kernel(at, *refs)

    return call(
        kernel,
        (sc, x, gain, *tables, *pieces),
        [SM] + [VM] * 4 + [ANY] * PIECES,
        (shaped((8, 2, 128, 384), BF), shaped((256, D), BF), shaped((256, D), BF)),
        [pltpu.VMEM((D, FF), BF), pltpu.SemaphoreType.DMA((8,))],
        2 * 256 * D * 960,
        5_000_000,
    )


def fill_padded(target, rows, first_row, first_lane):
    for g in range(KVH):
        for b in range(2):
            for h in range(3):
                head = 3 * g + h
                piece = rows[128 * b : 128 * b + 128, 64 * head : 64 * head + 64]
                zero = jnp.zeros_like(piece)
                pair = (piece, zero) if first_lane == 0 else (zero, piece)
                target[2 * g + b, first_row + 128 * h : first_row + 128 * h + 128] = (
                    jnp.concatenate(pair, axis=1).astype(BF)
                )


def slot_of(sc, i):
    pair = sc[2]
    is_low = i <= pair
    rank = jnp.where(is_low, sc[4 + min(i, 7)], sc[4 + lax.rem(8 - i + pair + 8, 8)])
    return is_low, 2 * rank + jnp.where(is_low, 0, 1)


def slots_of(sc):
    slots = []
    for i in range(9):
        is_low, block = slot_of(sc, i)
        slots.append((is_low, block, jnp.where(jnp.logical_or(i == sc[2], i == 8), 1.0, 0.0)))
    return slots + [(False, 2 * sc[4 + j], None) for j in range(8)]


def fill_mask(mask):
    key_at = lax.broadcasted_iota(jnp.int32, (128, 384), 0)
    query_at = lax.rem(lax.broadcasted_iota(jnp.int32, (128, 384), 1), 128)
    mask[...] = jnp.where(key_at <= query_at, 0.0, NEG)


def pick(is_low, low, high):
    if is_low is False:
        return high
    return jnp.where(is_low, low, high)


def add_to(is_low, low, high, value, combine):
    if is_low is False:
        return low, combine(high, value)
    return jnp.where(is_low, combine(low, value), low), jnp.where(is_low, high, combine(high, value))


def fill_turned(target, source, first_row):
    for at in range(6):
        target[at] = source[at, first_row : first_row + 384].astype(F32).T.astype(BF)


def attend_kernel(sc, q, held, out, log_total, padded, turned_q, scores, mask, heads):
    fill_padded(padded, q[...].astype(F32), 0, 0)
    fill_turned(turned_q, padded, 0)
    fill_mask(mask)
    slots = slots_of(sc)

    def key_head(g, carry):
        lanes = pl.ds(pl.multiple_of(128 * g, 128), 128)
        top_low = top_high = jnp.full((1, 384), NEG, F32)
        for k, (is_low, block, masked) in enumerate(slots):
            score = nn(held[block, :, lanes], turned_q[2 * g + pick(is_low, 0, 1)])
            if masked is not None:
                score = score + mask[...] * masked
            scores[k] = score
            top = jnp.max(score, axis=0, keepdims=True)
            top_low, top_high = add_to(is_low, top_low, top_high, top, jnp.maximum)
        total_low = total_high = jnp.zeros((1, 384), F32)
        rows_low = rows_high = jnp.zeros((HD, 384), F32)
        for k, (is_low, block, _) in enumerate(slots):
            expo = jnp.exp(scores[k] - pick(is_low, top_low, top_high))
            total = jnp.sum(expo, axis=0, keepdims=True)
            values = held[block, :, lanes].astype(F32).T[HD:].astype(BF)
            rows = nn(values, expo.astype(BF))
            total_low, total_high = add_to(is_low, total_low, total_high, total, jnp.add)
            rows_low, rows_high = add_to(is_low, rows_low, rows_high, rows, jnp.add)
        log_total[2 * g] = jnp.broadcast_to(top_low + jnp.log(total_low), (8, 384))
        log_total[2 * g + 1] = jnp.broadcast_to(top_high + jnp.log(total_high), (8, 384))
        heads[2 * g] = rows_low / total_low
        heads[2 * g + 1] = rows_high / total_high
        return carry

    lax.fori_loop(0, KVH, key_head, 0)
    for g in range(KVH):
        for b in range(2):
            turned = heads[2 * g + b].T.astype(BF)
            for h in range(3):
                head = 3 * g + h
                out[128 * b : 128 * b + 128, 64 * head : 64 * head + 64] = turned[
                    128 * h : 128 * h + 128
                ]


def attend(sc, q, kvs):
    return call(
        attend_kernel,
        (sc, q, kvs),
        [SM, VM, VM],
        (shaped((256, D), BF), shaped((6, 8, 384), F32)),
        [
            pltpu.VMEM((6, 384, 128), BF),
            pltpu.VMEM((6, 128, 384), BF),
            pltpu.VMEM((17, 128, 384), F32),
            pltpu.VMEM((128, 384), F32),
            pltpu.VMEM((6, HD, 384), F32),
        ],
        4 * 17 * 3 * 128 * 128 * 384,
        4_000_000,
    )


def attend_back_kernel(
    sc, q, rows_out, grad_out, log_total, cosine, sine, held, grad_q, grad_kv, both, delta, acc,
    early, slotted, dq, mask, probs, probs_low, grads_low, turned, turned_q, turned_g,
):
    fill_padded(both, q[...].astype(F32), 0, 0)
    fill_padded(both, grad_out[...].astype(F32), 384, 64)
    fill_turned(turned_q, both, 0)
    fill_turned(turned_g, both, 384)
    fill_mask(mask)
    product = rows_out[...].astype(F32) * grad_out[...].astype(F32)
    for g in range(KVH):
        for b in range(2):
            for h in range(3):
                head = 3 * g + h
                piece = product[128 * b : 128 * b + 128, 64 * head : 64 * head + 64]
                delta[2 * g + b, 0:1, 128 * h : 128 * h + 128] = jnp.sum(
                    piece.T, axis=0, keepdims=True
                )
    slots = slots_of(sc)

    def key_head(g, carry):
        lanes = pl.ds(pl.multiple_of(128 * g, 128), 128)
        for k, (is_low, block, masked) in enumerate(slots):
            at = 2 * g + pick(is_low, 0, 1)
            score = nn(held[block, :, lanes], turned_q[at])
            if masked is not None:
                score = score + mask[...] * masked
            prob = jnp.exp(score - log_total[at, 0:1])
            probs[k] = prob
            probs_low[k] = prob.astype(BF)
        for k, (is_low, block, _) in enumerate(slots):
            at = 2 * g + pick(is_low, 0, 1)
            tile = held[block, :, lanes]
            grad_prob = nn(tile, turned_g[at])
            grads_low[128 * k : 128 * k + 128] = (
                probs[k] * (grad_prob - delta[at, 0:1])
            ).astype(BF)
            turned[:, 128 * k : 128 * k + 128] = tile.astype(F32).T[:HD].astype(BF)
        low = jnp.zeros((HD, 384), F32)
        high = nn(turned[:, 1152:], grads_low[1152:])
        for k, (is_low, _, _) in enumerate(slots):
            at = 2 * g + pick(is_low, 0, 1)
            rows = slice(128 * k, 128 * k + 128)
            grad_score = grads_low[rows]
            if k < 9:
                low, high = add_to(is_low, low, high, nn(turned[:, rows], grad_score), jnp.add)
            pair = nn(grad_score, both[at, :384]) + nn(probs_low[k], both[at, 384:])
            if k < 9:
                slotted[k, :, lanes] = pair
            else:
                early[k - 9, :, lanes] = pair + jnp.where(
                    k - 9 <= sc[2], slotted[k - 9, :, lanes], 0.0
                )
        acc[2 * g] = low
        acc[2 * g + 1] = high
        return carry

    lax.fori_loop(0, KVH, key_head, 0)
    dq[...] = jnp.zeros_like(dq)
    for g in range(KVH):
        for b in range(2):
            heads = acc[2 * g + b].T
            for h in range(3):
                head = 3 * g + h
                dq[128 * b : 128 * b + 128, 64 * head : 64 * head + 64] = heads[
                    128 * h : 128 * h + 128
                ] * (HD**-0.5)
    turned = rope_back(
        dq[...], table_lanes(cosine[...], 1.0)[:, 384:], table_lanes(sine[...], 0.0)[:, 384:]
    )
    grad_q[...] = turned[:, :D].astype(BF)
    for r in range(8):
        pair = sc[13 + r]
        slot = 8 + sc[2] - pair
        grad_kv[2 * r] = early[pair].astype(BF)
        grad_kv[2 * r + 1] = jnp.where(
            slot <= 8, slotted[jnp.minimum(slot, 8)], 0.0
        ).astype(BF)


def attend_back(sc, q, rows_out, grad_out, log_total, tables, kvs):
    return call(
        attend_back_kernel,
        (sc, q, rows_out, grad_out, log_total, *tables, kvs),
        [SM] + [VM] * 7,
        (shaped((256, D), BF), shaped((16, 128, 384), BF)),
        [
            pltpu.VMEM((6, 768, 128), BF),
            pltpu.VMEM((6, 8, 384), F32),
            pltpu.VMEM((6, 64, 384), F32),
            pltpu.VMEM((8, 128, 384), F32),
            pltpu.VMEM((9, 128, 384), F32),
            pltpu.VMEM((256, 640), F32),
            pltpu.VMEM((128, 384), F32),
            pltpu.VMEM((17, 128, 384), F32),
            pltpu.VMEM((17, 128, 384), BF),
            pltpu.VMEM((17 * 128, 384), BF),
            pltpu.VMEM((HD, 17 * 128), BF),
            pltpu.VMEM((6, 128, 384), BF),
            pltpu.VMEM((6, 128, 384), BF),
        ],
        10 * 17 * 3 * 128 * 128 * 384,
        8_000_000,
    )


CHUNK = 512


def feed_kernel(x, rows_out, gain, copies, *refs):
    middle_out, normed_out, gate_out, up_out, after = refs[:5]
    weight, gate_w, up_w, down_w, _ = refs[5:]
    first, second, third = copies
    wait_all(first)
    middle = x[...] + nn(rows_out[...], weight[:, 960:])
    middle_out[...] = middle
    normed = (middle * norm_factor(middle) * gain[...]).astype(BF)
    normed_out[...] = normed
    wait_all(second)
    wait_all(third)
    total = middle
    for at in range(0, FF, CHUNK):
        gate = nn(normed, gate_w[:, at : at + CHUNK])
        up = nn(normed, up_w[:, at : at + CHUNK])
        gate_out[:, at : at + CHUNK] = gate
        up_out[:, at : at + CHUNK] = up
        hidden = (gate * jax.nn.sigmoid(gate) * up).astype(BF)
        total = total + nn(hidden, down_w[at : at + CHUNK, :D])
    after[...] = total


def feed(sc, x, rows_out, gain, c_pieces, m_pieces):
    c_pieces, m_pieces = c_pieces[0], m_pieces[0]
    n_m = len(m_pieces)

    def kernel(sc, x, rows_out, gain, *refs):
        c_refs, m_refs, refs = refs[:PIECES], refs[PIECES : PIECES + n_m], refs[PIECES + n_m :]
        copies = weight_copies(sc, c_refs, m_refs, refs[5:], False)
        feed_kernel(x, rows_out, gain, copies, *refs)

    wide = shaped((256, FF), F32)
    narrow = shaped((256, D), F32)
    return call(
        kernel,
        (sc, x, rows_out, gain, *c_pieces, *m_pieces),
        [SM] + [VM] * 3 + [ANY] * 2 * PIECES,
        (narrow, shaped((256, D), BF), wide, wide, narrow),
        [
            pltpu.VMEM((D, FF), BF),
            pltpu.VMEM((D, FF), BF),
            pltpu.VMEM((D, FF), BF),
            pltpu.VMEM((FF, HALF), BF),
            pltpu.SemaphoreType.DMA((32,)),
        ],
        2 * 256 * D * (D + 3 * FF),
        14_000_000,
    )


def weight_copies(sc, c_pieces, m_pieces, scratch, last_first):
    weight, gate_w, up_w, down_w, sems = scratch

    def square():
        return unit_copies(sc, c_pieces, 0, 144, weight, 144, False, sems, 0)

    first = None if last_first else square()
    third = unit_copies(sc, m_pieces, 288, 192, down_w, 384, True, sems, 24) if last_first else None
    second = unit_copies(sc, m_pieces, 0, 144, gate_w, 144, False, sems, 8)
    second += unit_copies(sc, m_pieces, 144, 144, up_w, 144, False, sems, 16)
    if third is None:
        third = unit_copies(sc, m_pieces, 288, 192, down_w, 384, True, sems, 24)
    return square() if first is None else first, second, third


def feed_back_kernel(upstream, middle, gate, up, gain, copies, *refs):
    grad_middle, grad_attn_out, grad_rows, grad_gate_out, grad_up_out, hidden_out, grad_gain = refs[
        :7
    ]
    weight, gate_w, up_w, down_w, _ = refs[7:]
    first, second, third = copies
    grad_down = upstream[...].astype(BF)
    wait_all(third)
    wait_all(second)
    grad_normed = jnp.zeros((256, D), F32)
    for at in range(0, FF, CHUNK):
        lanes = slice(at, at + CHUNK)
        grad_hidden = nt(grad_down, down_w[at : at + CHUNK, :D])
        gate_act, up_proj = gate[:, lanes], up[:, lanes]
        sigma = jax.nn.sigmoid(gate_act)
        silu = gate_act * sigma
        grad_gate = (grad_hidden * up_proj * sigma * (1.0 + gate_act * (1.0 - sigma))).astype(BF)
        grad_up = (grad_hidden * silu).astype(BF)
        grad_gate_out[:, lanes] = grad_gate
        grad_up_out[:, lanes] = grad_up
        hidden_out[:, lanes] = (silu * up_proj).astype(BF)
        grad_normed = grad_normed + nt(grad_gate, gate_w[:, lanes]) + nt(grad_up, up_w[:, lanes])
    back, grad_gain_sum = norm_back(middle[...], gain[...], grad_normed)
    grad_gain[...] = grad_gain_sum
    total = upstream[...] + back
    grad_middle[...] = total
    grad_attn = total.astype(BF)
    grad_attn_out[...] = grad_attn
    wait_all(first)
    grad_rows[...] = nt(grad_attn, weight[:, 960:]).astype(BF)


FEED_BACK_OUTS = (
    (shaped((256, D), F32),)
    + (shaped((256, D), BF),) * 2
    + (shaped((256, FF), BF),) * 3
    + (shaped((1, D), F32),)
)
FEED_SCRATCH = [pltpu.VMEM((D, FF), BF)] * 3 + [
    pltpu.VMEM((FF, HALF), BF),
    pltpu.SemaphoreType.DMA((32,)),
]


def feed_both(sc, x, rows_out, gain, upstream, c_pieces, m_pieces):
    c_pieces, m_pieces = c_pieces[0], m_pieces[0]
    n_m = len(m_pieces)

    def kernel(sc, x, rows_out, gain, upstream, *refs):
        c_refs, m_refs, refs = refs[:PIECES], refs[PIECES : PIECES + n_m], refs[PIECES + n_m :]
        mixed, normed_out, back_outs, refs = refs[0], refs[1], refs[2:9], refs[9:]
        middle, gate, up, after, *scratch = refs
        copies = weight_copies(sc, c_refs, m_refs, scratch, False)
        feed_kernel(
            x, rows_out, gain, copies, middle, normed_out, gate, up, after, *scratch
        )
        mixed[...] = after[...].T.astype(BF)
        feed_back_kernel(
            upstream, middle, gate, up, gain, ([], [], []), *back_outs, *scratch
        )

    return call(
        kernel,
        (sc, x, rows_out, gain, upstream, *c_pieces, *m_pieces),
        [SM] + [VM] * 4 + [ANY] * (PIECES + n_m),
        (shaped((D, 256), BF), shaped((256, D), BF)) + FEED_BACK_OUTS,
        [
            pltpu.VMEM((256, D), F32),
            pltpu.VMEM((256, FF), F32),
            pltpu.VMEM((256, FF), F32),
            pltpu.VMEM((256, D), F32),
        ]
        + FEED_SCRATCH,
        4 * 256 * D * (D + 3 * FF),
        14_000_000,
    )


def store_piece(sc, parts, owner, half, rows, value, own_first=True):
    slot = lax.rem(owner - sc[0] + 4, 4) if own_first else owner
    parts[jnp.where(sc[1] == half, 0, 1), slot, rows] = value


def send_parts(parts, keep, send, sems):
    copies = [
        pltpu.make_async_copy(parts.at[k], ref, sems.at[k]) for k, ref in enumerate((keep, send))
    ]
    for copy in copies:
        copy.start()
    wait_all(copies)


def parts_scratch(rows):
    return [pltpu.VMEM((2, 4, rows, HALF), BF), pltpu.SemaphoreType.DMA((2,))]


def feed_grads_kernel(sc, normed, grad_gate, grad_up, hidden, upstream, keep, send, turned, tall, *held):
    turned[...] = normed[...].astype(F32).T.astype(BF)
    for at in range(0, FF, CHUNK):
        tall[at : at + CHUNK] = hidden[:, at : at + CHUNK].astype(F32).T.astype(BF)
    grad_down = jnp.concatenate(
        [upstream[...], jnp.zeros((256, HALF - D), F32)], axis=1
    ).astype(BF)
    for half in range(2):
        lanes = slice(HALF * half, HALF * half + HALF)
        for owner in range(4):
            left = turned[144 * owner : 144 * owner + 144]
            at = 384 * owner + 192 * half
            for rows, value in (
                (slice(0, 144), nn(left, grad_gate[:, lanes])),
                (slice(144, 288), nn(left, grad_up[:, lanes])),
                (slice(288, 480), nn(tall[at : at + 192], grad_down)),
            ):
                store_piece(sc, held[0], owner, half, rows, value.astype(BF))
    send_parts(held[0], keep, send, held[1])


def feed_grads(sc, normed, grad_gate, grad_up, hidden, upstream):
    out = shaped((4, MROWS, HALF), BF)
    return call(
        feed_grads_kernel,
        (sc, normed, grad_gate, grad_up, hidden, upstream),
        [SM] + [VM] * 5,
        (out, out),
        [pltpu.VMEM((D, 256), BF), pltpu.VMEM((FF, 256), BF)] + parts_scratch(MROWS),
        2 * 256 * D * 3 * FF,
        9_000_000,
        2,
    )


def grad_kv_rows(grad_kvs, cosine, sine, half):
    total = grad_kvs[0, half].astype(F32)
    for r in range(1, 8):
        total = total + grad_kvs[r, half].astype(F32)
    rows = slice(128 * half, 128 * half + 128)
    cos_t, sin_t = table_lanes(cosine[rows], 1.0), table_lanes(sine[rows], 0.0)
    return rope_back(total, cos_t[:, :384], sin_t[:, :384])


def project_back_kernel(
    sc, x, gain, cosine, sine, grad_middle, grad_q, normed, attn_rows, grad_attn, gain_two,
    grad_kvs, *refs,
):
    pieces, (upstream, keep, send, weight, buf, turned, sems, *held) = (
        refs[:PIECES], refs[PIECES:]
    )
    copies = unit_copies(sc, pieces, 0, 144, weight, 144, False, sems, 0)
    for half in range(2):
        rows = slice(128 * half, 128 * half + 128)
        buf[rows, :384] = grad_kv_rows(grad_kvs, cosine, sine, half)
    buf[:, 384:960] = grad_q[...].astype(F32)
    buf[:, 960:] = grad_attn[...].astype(F32)
    inner = buf[:, :960].astype(BF)
    wait_all(copies)
    grad_normed = nt(inner, weight[:, :960])
    back, grad_gain = norm_back(x[...], gain[...], grad_normed)
    upstream[...] = grad_middle[...] + back
    turned[0] = normed[...].astype(F32).T.astype(BF)
    turned[1] = attn_rows[...].astype(F32).T.astype(BF)
    right = [buf[:, :HALF].astype(BF), buf[:, HALF:].astype(BF)]
    lane = lax.broadcasted_iota(jnp.int32, (144, HALF), 1)
    gains = (grad_gain, gain_two[...])
    for owner in range(4):
        rows = slice(144 * owner, 144 * owner + 144)
        for half in range(2):
            value = nn(turned[0, rows], right[half])
            if half == 1:
                value = jnp.where(lane < 192, value, nn(turned[1, rows], right[1]))
            store_piece(sc, held[0], owner, half, slice(0, 144), value.astype(BF), False)
            row = jnp.concatenate([gains[half][:, rows], jnp.zeros((1, HALF - 144), F32)], axis=1)
            block = jnp.broadcast_to(row, (16, HALF))
            store_piece(sc, held[0], owner, half, slice(144, 160), block.astype(BF), False)
    send_parts(held[0], keep, send, held[1])


def between_layers(
    sc, x, gain, tables, grad_middle, grad_q, normed, attn_rows, grad_attn, gain_two, grad_kvs,
    pieces, middle, gate, up, gain_below, c_pieces, m_pieces,
):
    pieces, c_pieces, m_pieces = pieces[0], c_pieces[0], m_pieces[0]
    n_m = len(m_pieces)

    def kernel(sc, *refs):
        ins, refs = refs[:11], refs[11:]
        below, refs = refs[:4], refs[4:]
        mine, c_refs, refs = refs[:PIECES], refs[PIECES : 2 * PIECES], refs[2 * PIECES :]
        m_refs, refs = refs[:n_m], refs[n_m:]
        upstream, back_outs, keep, send, refs = refs[0], refs[1:8], refs[8], refs[9], refs[10:]
        scratch = refs[6:]
        copies = weight_copies(sc, c_refs, m_refs, scratch, True)
        project_back_kernel(sc, *ins, *mine, upstream, keep, send, *refs[:6])
        feed_back_kernel(upstream, *below, copies, *back_outs, *scratch)

    out = shaped((4, CROWS, HALF), BF)
    return call(
        kernel,
        (
            sc, x, gain, *tables, grad_middle, grad_q, normed, attn_rows, grad_attn, gain_two,
            grad_kvs, middle, gate, up, gain_below, *pieces, *c_pieces, *m_pieces,
        ),
        [SM] + [VM] * 15 + [ANY] * (2 * PIECES + n_m),
        (shaped((256, D), F32),) + FEED_BACK_OUTS + (out, out),
        [
            pltpu.VMEM((D, FF), BF),
            pltpu.VMEM((256, FF), F32),
            pltpu.VMEM((2, D, 256), BF),
            pltpu.SemaphoreType.DMA((8,)),
        ]
        + parts_scratch(CROWS)
        + FEED_SCRATCH,
        2 * 256 * D * (960 + 2 * FF),
        20_000_000,
        2,
    )


def early_grads_kernel(sc, normed, grad_q, attn_rows, grad_attn, keep, send, turned, *held):
    turned[0] = normed[...].astype(F32).T.astype(BF)
    turned[1] = attn_rows[...].astype(F32).T.astype(BF)
    for half, right in enumerate((grad_q, grad_attn)):
        for owner in range(4):
            value = nn(turned[half, 144 * owner : 144 * owner + 144], right[...])
            value = jnp.concatenate([value, jnp.zeros((144, HALF - D), F32)], axis=1)
            value = jnp.concatenate([value, jnp.zeros((16, HALF), F32)], axis=0)
            store_piece(sc, held[0], owner, half, slice(0, CROWS), value.astype(BF))
    send_parts(held[0], keep, send, held[1])


def early_grads(sc, normed, grad_q, attn_rows, grad_attn):
    out = shaped((4, CROWS, HALF), BF)
    return call(
        early_grads_kernel,
        (sc, normed, grad_q, attn_rows, grad_attn),
        [SM] + [VM] * 4,
        (out, out),
        [pltpu.VMEM((2, D, 256), BF)] + parts_scratch(CROWS),
        4 * 256 * D * D,
        4_000_000,
        2,
    )


LROWS = 80


def late_back_kernel(
    at, sc, x, gain, cosine, sine, grad_middle, grad_q, normed, gain_two, grad_kvs, *refs
):
    pieces, (grad_tokens, parts, weight, buf, turned, sems) = refs[:PIECES], refs[PIECES:]
    copies = unit_copies(sc, pieces, at, 144, weight, 144, False, sems, 0)
    for half in range(2):
        rows = slice(128 * half, 128 * half + 128)
        buf[rows, :384] = grad_kv_rows(grad_kvs, cosine, sine, half).astype(BF)
    buf[:, 384:] = grad_q[...]
    wait_all(copies)
    grad_normed = nt(buf[...], weight[:, :960])
    back, grad_gain = norm_back(x[...], gain[...], grad_normed)
    grad_tokens[...] = (grad_middle[...] + back).T.astype(BF)
    turned[...] = normed[...].astype(F32).T.astype(BF)
    gains = (grad_gain, gain_two[...])
    for owner in range(4):
        rows = slice(144 * owner, 144 * owner + 144)
        value = nn(turned[rows], buf[:, :384])
        for half in range(2):
            row = jnp.concatenate([gains[half][:, rows], jnp.zeros((1, 384 - 144), F32)], axis=1)
            block = jnp.broadcast_to(row, (8, 384))
            piece = jnp.concatenate([value[72 * half : 72 * half + 72], block], axis=0)
            parts[4 * half + owner] = piece.astype(BF)


def late_back(sc, x, gain, tables, grad_middle, grad_q, normed, gain_two, grad_kvs, pieces):
    pieces, at = pieces

    def kernel(*refs):
        late_back_kernel(at, *refs)

    return call(
        kernel,
        (sc, x, gain, *tables, grad_middle, grad_q, normed, gain_two, grad_kvs, *pieces),
        [SM] + [VM] * 9 + [ANY] * PIECES,
        (shaped((D, 256), BF), shaped((8, LROWS, 384), BF)),
        [
            pltpu.VMEM((D, FF), BF),
            pltpu.VMEM((256, 960), BF),
            pltpu.VMEM((D, 256), BF),
            pltpu.SemaphoreType.DMA((8,)),
        ],
        2 * 256 * D * (960 + 384),
        6_000_000,
    )


def halves_in_order(sc, mine, other):
    rows = mine[...].astype(F32), other[...].astype(F32)
    is_first = sc[1] == 0
    return jnp.where(is_first, rows[0], rows[1]), jnp.where(is_first, rows[1], rows[0])


def in_order(sc, mine, other, spread):
    first = MROWS // 4
    second = mine.shape[1] - first
    for k in range(4):
        slot = lax.rem(sc[12] + k, 4)
        at_first = pl.ds(pl.multiple_of(slot * first, 8), first)
        at_second = pl.ds(pl.multiple_of(MROWS + slot * second, 8), second)
        for side, ref in enumerate((mine, other)):
            spread[side, at_first] = ref[k, :first].astype(F32)
            spread[side, at_second] = ref[k, first:].astype(F32)
    return spread.at[sc[1]], spread.at[1 - sc[1]]


def heads_apart(rows):
    keys = [rows[:, 128 * g : 128 * g + HD] for g in range(KVH)]
    values = [rows[:, 128 * g + HD : 128 * g + 128] for g in range(KVH)]
    return jnp.concatenate(keys, axis=1), jnp.concatenate(values, axis=1)


def place_all(pairs, sems, layer):
    copies = [
        pltpu.make_async_copy(src, dst.at[layer], sems.at[k]) for k, (src, dst) in enumerate(pairs)
    ]
    for copy in copies:
        copy.start()
    return copies


def fill_wide(left, right, at, gate, up, down):
    for k, rows in enumerate((left, right)):
        lanes = slice(HALF * k, HALF * k + HALF)
        gate[:, lanes] = rows[at : at + 144]
        up[:, lanes] = rows[at + 144 : at + 288]
    halves = [rows[at + 288 : at + 480, :D] for rows in (left, right)]
    down[...] = jnp.concatenate(halves, axis=0).T


def fill_square(left, right, at, query, out, key, value):
    query[:, :384], query[:, 384:] = left[at : at + 144, 384:], right[at : at + 144, :192]
    out[...] = right[at : at + 144, 192:]
    key[...], value[...] = heads_apart(left[at : at + 144, :384])


def assemble_kernel(sc, mine, other, e_mine, e_other, l_mine, l_other, *refs):
    (gain_a, gain_b), outs, held, spread, sems = refs[:2], refs[2:9], refs[9:23], refs[23], refs[24]
    left, right = in_order(sc, mine, other, spread)
    fill_wide(left, right, 0, *held[:3])
    copies = place_all(zip(held[:3], outs[:3]), sems, 1)
    fill_wide(left, right, MROWS + CROWS, *held[3:6])
    copies += place_all(zip(held[3:6], outs[:3]), sems.at[pl.ds(3, 3)], 0)
    fill_square(left, right, MROWS, *held[6:10])
    copies += place_all(zip(held[6:10], outs[3:]), sems.at[pl.ds(6, 4)], 1)
    row = MROWS + 144
    gain_a[1:2], gain_b[1:2] = left[row : row + 1, :144], right[row : row + 1, :144]
    query, out, key, value = held[10:]
    left, right = halves_in_order(sc, e_mine, e_other)
    query[...], out[...] = left[:144, :D], right[:144, :D]
    left, right = halves_in_order(sc, l_mine, l_other)
    key[...], value[...] = heads_apart(jnp.concatenate([left[:72], right[:72]], axis=0))
    gain_a[0:1], gain_b[0:1] = left[72:73, :144], right[72:73, :144]
    copies += place_all(zip(held[10:], outs[3:]), sems.at[pl.ds(10, 4)], 0)
    wait_all(copies)


PLACED = ((144, FF),) * 2 + ((D, 384),) + ((144, D),) * 2 + ((144, KVH * HD),) * 2


def assemble(*ins):
    held = PLACED[:3] + PLACED[:3] + PLACED[3:] + PLACED[3:]
    return pl.pallas_call(
        assemble_kernel,
        out_shape=(shaped((LAYERS, 144), F32),) * 2
        + tuple(shaped((LAYERS,) + shape, F32) for shape in PLACED),
        in_specs=[SM] + [VM] * (len(ins) - 1),
        out_specs=[VM] * 2 + [ANY] * len(PLACED),
        scratch_shapes=[pltpu.VMEM(shape, F32) for shape in held]
        + [
            pltpu.VMEM((2, 4 * ins[1].shape[1], HALF), F32),
            pltpu.SemaphoreType.DMA((len(held),)),
        ],
        compiler_params=pltpu.CompilerParams(vmem_limit_bytes=VMEM_LIMIT),
        cost_estimate=pl.CostEstimate(flops=1000, bytes_accessed=1000, transcendentals=0),
    )(*ins)


def ring(axis, shift):
    n = lax.axis_size(axis)
    return [(i, (i + shift) % n) for i in range(n)]


def swap_core(value):
    return lax.ppermute(value, "core", [(0, 1), (1, 0)])


def all_pairs(value, axis):
    return lax.all_to_all(value, axis, 0, 0, tiled=True)


def copied(value, n):
    return jnp.broadcast_to(value[None], (n,) + value.shape)


def added(parts):
    total = parts[0].astype(F32)
    for part in parts[1:]:
        total = total + part.astype(F32)
    return total


def summed_rows(pieces, n):
    return added([pieces[k] for k in range(n)])


def around(own, axis):
    own = own.astype(BF)
    return added([own] + [lax.ppermute(own, axis, ring(axis, s)) for s in (1, 2, 3)])


def phase(*values):
    return lax.optimization_barrier(values)


def sent(pieces, shifts):
    return [lax.ppermute(pieces[k], "fsdp", ring("fsdp", k)) for k in shifts]


def near(mine, shifts):
    return [lax.ppermute(mine, "fsdp", ring("fsdp", -k)) for k in shifts]


def gathered(quarter, shifts):
    return [lax.ppermute(quarter, "dp", ring("dp", -k)) for k in shifts]


def swap_all(parts):
    return [swap_core(part) for part in parts]


def joined(parts):
    return [
        jnp.concatenate([added([keep[k], got[k]]).astype(BF) for keep, got in parts], axis=0)
        for k in range(4)
    ]


def quarters(total):
    return total.astype(BF).reshape(4, -1, HALF)


def halves_of(full):
    return jnp.stack([full[:, :HALF], full[:, HALF:]])


def of_core(own, core):
    return lax.dynamic_index_in_dim(own, core, 0, keepdims=False)


def local(
    tokens, pair_order, cotangent, norm_first, w_query, w_key, w_value, w_out, norm_second,
    w_gate, w_up, w_down,
):
    core = lax.axis_index("core")
    rank = lax.axis_index("x") * 2 + core
    y = lax.axis_index("fsdp")
    order = pair_order[0]
    my_pair = lax.dynamic_index_in_dim(order, rank, 0, keepdims=False)
    ids = jnp.arange(8, dtype=jnp.int32)
    inverse = jnp.sum(jnp.where(order[None, :] == ids[:, None], ids[None, :], 0), axis=1)
    sc = jnp.concatenate(
        [
            jnp.stack([y, core, my_pair, rank]).astype(jnp.int32),
            inverse.astype(jnp.int32),
            lax.axis_index("dp").astype(jnp.int32)[None],
            order.astype(jnp.int32),
        ]
    )

    offsets = jnp.arange(256, dtype=jnp.int32)
    pos = jnp.where(
        offsets < 128, my_pair * 128 + offsets, (15 - my_pair) * 128 + offsets - 128
    )
    freq = jnp.power(THETA, -2.0 * (jnp.arange(128) % 32).astype(F32) / HD)
    angle = pos.astype(F32)[:, None] * freq
    tables = (jnp.cos(angle), jnp.sin(angle))

    gain_rows = jnp.pad(
        jnp.stack([norm_first[0], norm_second[0], norm_first[1], norm_second[1]]),
        ((0, 12), (0, HALF - 144)),
    )
    def c_slices(layer):
        cols = []
        for g in range(KVH):
            cols += [w_key[layer][:, 64 * g : 64 * g + 64], w_value[layer][:, 64 * g : 64 * g + 64]]
        full = jnp.concatenate(cols + [w_query[layer], w_out[layer]], axis=1)
        return jnp.concatenate(
            [halves_of(full), jnp.broadcast_to(gain_rows, (2, 16, HALF))], axis=1
        )

    def m_slices(gate, up, down):
        down = jnp.pad(down.reshape(2, 192, D), ((0, 0), (0, 0), (0, HALF - D)))
        return jnp.concatenate([halves_of(gate), halves_of(up), down], axis=1)

    own_c = c_slices(0)
    mine_c = of_core(own_c, core)
    own_b = m_slices(w_gate[0], w_up[0], w_down[0])
    mine_b = of_core(own_b, core)
    near_c = near(mine_c, (1, 2, 3))
    far_c = swap_all(near_c)
    gains = jnp.stack([mine_c[144:148, :144]] + [part[144:148, :144] for part in near_c])
    gains = jnp.roll(gains, y, axis=0).transpose(1, 0, 2).reshape(4, 1, D).astype(F32)
    gain_one, gain_two = (gains[0], gains[2]), (gains[1], gains[3])
    c_zero = ((own_c, *near_c, *far_c), 0)

    x = tokens[0].astype(F32)
    b1, b3 = near(mine_b, (1, 3))
    kv, q, normed = project(sc, x, gain_one[0], tables, c_zero)
    kv, b1, b3, mine_b, *late_w = phase(kv, b1, b3, mine_b, w_gate[1], w_up[1], w_down[1])
    (b2,) = near(mine_b, (2,))
    f1, f3 = swap_all((b1, b3))
    kvs = all_pairs(kv, ("x", "core")).reshape(16, 128, 384)
    own_d, own_m = c_slices(1), m_slices(*late_w)
    mine_d, mine_m = of_core(own_d, core), of_core(own_m, core)
    kvs, b2, f1, f3, mine_d, own_d, mine_m, own_m = phase(
        kvs, b2, f1, f3, mine_d, own_d, mine_m, own_m
    )
    f2 = swap_core(b2)
    near_d = near(mine_d, (1, 2, 3))
    rows_out, log_total = attend(sc, q, kvs)
    rows_out, f2, mine_m, *near_d = phase(rows_out, f2, mine_m, *near_d)
    m_zero = ((own_b, b1, b2, b3, f1, f2, f3), 0)
    c_one = ((own_d, *near_d, *swap_all(near_d)), 0)
    m1, m3 = near(mine_m, (1, 3))
    middle, normed_two, gate, up, after = feed(sc, x, rows_out, gain_two[0], c_zero, m_zero)
    saved = [(x, kvs, q, normed, rows_out, log_total, middle, normed_two, gate, up)]

    x = after
    kv, q, normed = project(sc, x, gain_one[1], tables, c_one)
    kv, m1, m3, mine_m = phase(kv, m1, m3, mine_m)
    (m2,) = near(mine_m, (2,))
    f1, f3 = swap_all((m1, m3))
    kvs = all_pairs(kv, ("x", "core")).reshape(16, 128, 384)
    kvs, m2, f1, f3 = phase(kvs, m2, f1, f3)
    f2 = swap_core(m2)
    rows_out, log_total = attend(sc, q, kvs)
    m_one = ((own_m, m1, m2, m3, f1, f2, f3), 0)
    upstream = cotangent[0].astype(F32)
    (
        mixed, normed_two, grad_middle, grad_attn, grad_rows, grad_gate, grad_up, hidden,
        grad_gain_two,
    ) = feed_both(sc, x, rows_out, gain_two[1], upstream, c_one, m_one)

    keep_m, send_m = feed_grads(sc, normed_two, grad_gate, grad_up, hidden, upstream)
    grad_rows, send_m = phase(grad_rows, send_m)
    got_m = swap_core(send_m)
    grad_q, grad_kvs = attend_back(sc, q, rows_out, grad_rows, log_total, tables, kvs)
    last = joined([(keep_m, got_m)])
    grad_kvs, *last = phase(grad_kvs, *last)
    l1, l3 = sent(last, (1, 3))
    grad_kvs = all_pairs(grad_kvs.reshape(8, 2, 128, 384), ("x", "core"))
    grad_kvs, l1, l3, *last = phase(grad_kvs, l1, l3, *last)
    (l2,) = sent(last, (2,))
    x_one, q_one, normed_one, rows_one = x, q, normed, rows_out
    x, kvs, q, normed, rows_out, log_total, middle, normed_two, gate, up = saved[0]
    (
        upstream, grad_middle, grad_attn, grad_rows, grad_gate, grad_up, hidden, grad_gain_two,
        keep_c, send_c,
    ) = between_layers(
        sc, x_one, gain_one[1], tables, grad_middle, grad_q, normed_one, rows_one, grad_attn,
        grad_gain_two, grad_kvs, c_one, middle, gate, up, gain_two[0], c_zero, m_zero,
    )

    last = quarters(added([last[0], l1, l2, l3]))
    grad_gate, send_c, last = phase(grad_gate, send_c, last)
    last = all_pairs(last, "dp")
    got_c = swap_core(send_c)
    keep_m, send_m = feed_grads(sc, normed_two, grad_gate, grad_up, hidden, upstream)
    last = summed_rows(last, 4)
    grad_rows, send_m, last, got_c = phase(grad_rows, send_m, last, got_c)
    middle_c = all_pairs(added([keep_c, got_c]).astype(BF), "fsdp")
    got_m = swap_core(send_m)
    last = around(last, "x").astype(BF)
    grad_q, grad_kvs = attend_back(sc, q, rows_out, grad_rows, log_total, tables, kvs)
    first = joined([(keep_m, got_m)])
    grad_kvs, grad_q, last, middle_c, *first = phase(grad_kvs, grad_q, last, middle_c, *first)
    f1, f2, f3 = sent(first, (1, 2, 3))
    (a2,) = gathered(last, (2,))
    grad_kvs = all_pairs(grad_kvs.reshape(8, 2, 128, 384), ("x", "core"))
    keep_e, send_e = early_grads(sc, normed, grad_q, rows_out, grad_attn)
    early = joined([(keep_e, swap_core(send_e))])
    first = quarters(
        jnp.concatenate([summed_rows(middle_c, 4), added([first[0], f1, f2, f3])], axis=0)
    )
    grad_kvs, first, last, a2, *early = phase(grad_kvs, first, last, a2, *early)
    first = all_pairs(first, "dp")
    a1, a3 = gathered(last, (1, 3))
    e1, e2, e3 = sent(early, (1, 2, 3))
    grad_tokens, late = late_back(
        sc, x, gain_one[0], tables, grad_middle, grad_q, normed, grad_gain_two, grad_kvs, c_zero
    )

    early = added([early[0], e1, e2, e3]).astype(BF)
    first = summed_rows(first, 4).astype(BF)
    late, first, early, a1, a3 = phase(late, first, early, a1, a3)
    late = summed_rows(all_pairs(late, ("core", "fsdp")), 8).astype(BF)
    first = around(first, "x").astype(BF)
    early = around(early, "dp").astype(BF)
    late, first, early = phase(late, first, early)
    joint = jnp.concatenate([early, late.reshape(LROWS // 2, HALF)], axis=0)
    joint = summed_rows(all_pairs(copied(joint, 4), "x"), 4).astype(BF)
    b1, b2, b3 = gathered(first, (1, 2, 3))
    first = jnp.concatenate(
        [jnp.stack([last, a1, a2, a3]), jnp.stack([first, b1, b2, b3])], axis=1
    )
    joint, first = phase(joint, first)
    early, late = joint[:CROWS], joint[CROWS:]
    late = around(late, "dp").astype(BF)
    first, early = (first, swap_core(first)), (early, swap_core(early))
    late, first, early = phase(late, first, early)
    late = late.reshape(LROWS, 384)
    gain_a, gain_b, gate, up, down, query, out, key, value = assemble(
        sc, *first, *early, late, swap_core(late)
    )
    return (
        mixed.T[None], grad_tokens.T[None], gain_a, query, key, value, out, gain_b, gate, up,
        down.transpose(0, 2, 1),
    )


def solution(mesh):
    split = jax.sharding.Mesh(mesh.devices.reshape(4, 4, 2, 4), ("dp", "x", "core", "fsdp"))
    rows = P(("dp", "fsdp"), ("x", "core"), None)
    flat, deep = P(None, "fsdp"), P(None, "fsdp", None)
    return jax.shard_map(
        local,
        mesh=split,
        in_specs=(rows, P(("dp", "fsdp"), None), rows, flat) + (deep,) * 4 + (flat,) + (deep,) * 3,
        out_specs=(rows, rows, flat) + (deep,) * 4 + (flat,) + (deep,) * 3,
        check_vma=False,
    )
```

```python
import jax
import jax.numpy as jnp
from jax import lax
from jax.experimental import pallas as pl
from jax.experimental.pallas import tpu as pltpu
from jax.sharding import PartitionSpec as P

NH = 9
KVH = 3
HD = 64
LAYERS = 2
D = 576
FF = 1536
HALF = 768
EPS = 1e-05
THETA = 100000.0
NEG = -1e30
BF = jnp.bfloat16
F32 = jnp.float32
CROWS = 160
MROWS = 480
VMEM_LIMIT = 60 * 1024 * 1024

ANY = pl.BlockSpec(memory_space=pl.ANY)
VM = pl.BlockSpec(memory_space=pltpu.VMEM)
SM = pl.BlockSpec(memory_space=pltpu.SMEM)


def nt(a, b):
    return lax.dot_general(a, b, (((1,), (1,)), ((), ())), preferred_element_type=F32)


def nn(a, b):
    return jnp.dot(a, b, preferred_element_type=F32)


def shaped(shape, dtype):
    return jax.ShapeDtypeStruct(shape, dtype)


def call(kernel, ins, specs, outs, scratch, flops, nbytes, far=0):
    return pl.pallas_call(
        kernel,
        out_shape=outs,
        in_specs=specs,
        out_specs=[VM] * (len(outs) - far) + [ANY] * far,
        scratch_shapes=scratch,
        compiler_params=pltpu.CompilerParams(vmem_limit_bytes=VMEM_LIMIT),
        cost_estimate=pl.CostEstimate(flops=1000, bytes_accessed=1000, transcendentals=0),
    )(*ins)


PIECES = 7


def unit_copies(sc, pieces, row, rows, dst, stride, split_rows, sems, first):
    core = sc[1]
    copies = []

    def add(src, slot, half):
        if split_rows:
            at = pl.multiple_of(slot * stride + half * (stride // 2), 16)
            target = dst.at[pl.ds(at, rows)]
        else:
            lanes = pl.ds(pl.multiple_of(half * HALF, 128), HALF)
            target = dst.at[pl.ds(pl.multiple_of(slot * stride, 16), rows), lanes]
        copies.append(pltpu.make_async_copy(src, target, sems.at[first + len(copies)]))

    for half in range(2):
        add(pieces[0].at[half, pl.ds(row, rows)], sc[0], half)
    for k in range(3):
        slot = lax.rem(sc[0] + k + 1, 4)
        add(pieces[1 + k].at[pl.ds(row, rows)], slot, core)
        add(pieces[4 + k].at[pl.ds(row, rows)], slot, 1 - core)
    for copy in copies:
        copy.start()
    return copies


def wait_all(copies):
    for copy in copies:
        copy.wait()


def lane_low(shape):
    return lax.rem(lax.broadcasted_iota(jnp.int32, shape, 1), 64) < 32


def rope(values, cosine, sine):
    width = values.shape[1]
    up = pltpu.roll(values, width - 32, 1)
    down = pltpu.roll(values, 32, 1)
    return values * cosine + jnp.where(lane_low(values.shape), -up, down) * sine


def rope_back(values, cosine, sine):
    width = values.shape[1]
    spun = values * sine
    up = pltpu.roll(spun, width - 32, 1)
    down = pltpu.roll(spun, 32, 1)
    return values * cosine + jnp.where(lane_low(values.shape), up, -down)


def table_lanes(narrow, kv_fill):
    first = lax.broadcasted_iota(jnp.int32, narrow.shape, 1) < HD
    pair = jnp.where(first, narrow, kv_fill)
    return jnp.concatenate([pair] * 3 + [narrow] * 4 + [jnp.where(first, narrow, 0.0)], axis=1)


def norm_factor(rows):
    return lax.rsqrt(jnp.mean(rows * rows, axis=-1, keepdims=True) + EPS)


def norm_back(rows, gain, upstream):
    factor = norm_factor(rows)
    scaled = upstream * gain
    inner = jnp.mean(scaled * rows, axis=-1, keepdims=True)
    grad_in = factor * scaled - rows * (factor * factor * factor) * inner
    return grad_in, jnp.sum(upstream * rows * factor, axis=0, keepdims=True)


def project_kernel(at, sc, x, gain, cosine, sine, *refs):
    pieces, (kv, q, normed_out, weight, sems) = refs[:PIECES], refs[PIECES:]
    copies = unit_copies(sc, pieces, at, 144, weight, 144, False, sems, 0)
    rows = x[...]
    normed = (rows * norm_factor(rows) * gain[...]).astype(BF)
    normed_out[...] = normed
    wait_all(copies)
    raw = nn(normed, weight[:, :1024])
    turned = rope(raw, table_lanes(cosine[...], 1.0), table_lanes(sine[...], 0.0))
    for s in range(8):
        kv[s, 0] = turned[:128, :384].astype(BF)
        kv[s, 1] = turned[128:, :384].astype(BF)
    q[...] = (turned[:, 384:960] * (HD**-0.5)).astype(BF)


def project(sc, x, gain, tables, pieces):
    pieces, at = pieces

    def kernel(*refs):
        project_kernel(at, *refs)

    return call(
        kernel,
        (sc, x, gain, *tables, *pieces),
        [SM] + [VM] * 4 + [ANY] * PIECES,
        (shaped((8, 2, 128, 384), BF), shaped((256, D), BF), shaped((256, D), BF)),
        [pltpu.VMEM((D, FF), BF), pltpu.SemaphoreType.DMA((8,))],
        2 * 256 * D * 960,
        5_000_000,
    )


def fill_padded(target, rows, first_row, first_lane):
    for g in range(KVH):
        for b in range(2):
            for h in range(3):
                head = 3 * g + h
                piece = rows[128 * b : 128 * b + 128, 64 * head : 64 * head + 64]
                zero = jnp.zeros_like(piece)
                pair = (piece, zero) if first_lane == 0 else (zero, piece)
                target[2 * g + b, first_row + 128 * h : first_row + 128 * h + 128] = (
                    jnp.concatenate(pair, axis=1).astype(BF)
                )


def slot_of(sc, i):
    pair = sc[2]
    is_low = i <= pair
    rank = jnp.where(is_low, sc[4 + min(i, 7)], sc[4 + lax.rem(8 - i + pair + 8, 8)])
    return is_low, 2 * rank + jnp.where(is_low, 0, 1)


def slots_of(sc):
    slots = []
    for i in range(9):
        is_low, block = slot_of(sc, i)
        slots.append((is_low, block, jnp.where(jnp.logical_or(i == sc[2], i == 8), 1.0, 0.0)))
    return slots + [(False, 2 * sc[4 + j], None) for j in range(8)]


def fill_mask(mask):
    key_at = lax.broadcasted_iota(jnp.int32, (128, 384), 0)
    query_at = lax.rem(lax.broadcasted_iota(jnp.int32, (128, 384), 1), 128)
    mask[...] = jnp.where(key_at <= query_at, 0.0, NEG)


def pick(is_low, low, high):
    if is_low is False:
        return high
    return jnp.where(is_low, low, high)


def add_to(is_low, low, high, value, combine):
    if is_low is False:
        return low, combine(high, value)
    return jnp.where(is_low, combine(low, value), low), jnp.where(is_low, high, combine(high, value))


def fill_turned(target, source, first_row):
    for at in range(6):
        target[at] = source[at, first_row : first_row + 384].astype(F32).T.astype(BF)


def attend_kernel(sc, q, held, out, log_total, padded, turned_q, scores, mask, heads):
    fill_padded(padded, q[...].astype(F32), 0, 0)
    fill_turned(turned_q, padded, 0)
    fill_mask(mask)
    slots = slots_of(sc)

    def key_head(g, carry):
        lanes = pl.ds(pl.multiple_of(128 * g, 128), 128)
        top_low = top_high = jnp.full((1, 384), NEG, F32)
        for k, (is_low, block, masked) in enumerate(slots):
            score = nn(held[block, :, lanes], turned_q[2 * g + pick(is_low, 0, 1)])
            if masked is not None:
                score = score + mask[...] * masked
            scores[k] = score
            top = jnp.max(score, axis=0, keepdims=True)
            top_low, top_high = add_to(is_low, top_low, top_high, top, jnp.maximum)
        total_low = total_high = jnp.zeros((1, 384), F32)
        rows_low = rows_high = jnp.zeros((HD, 384), F32)
        for k, (is_low, block, _) in enumerate(slots):
            expo = jnp.exp(scores[k] - pick(is_low, top_low, top_high))
            total = jnp.sum(expo, axis=0, keepdims=True)
            values = held[block, :, lanes].astype(F32).T[HD:].astype(BF)
            rows = nn(values, expo.astype(BF))
            total_low, total_high = add_to(is_low, total_low, total_high, total, jnp.add)
            rows_low, rows_high = add_to(is_low, rows_low, rows_high, rows, jnp.add)
        log_total[2 * g] = jnp.broadcast_to(top_low + jnp.log(total_low), (8, 384))
        log_total[2 * g + 1] = jnp.broadcast_to(top_high + jnp.log(total_high), (8, 384))
        heads[2 * g] = rows_low / total_low
        heads[2 * g + 1] = rows_high / total_high
        return carry

    lax.fori_loop(0, KVH, key_head, 0)
    for g in range(KVH):
        for b in range(2):
            turned = heads[2 * g + b].T.astype(BF)
            for h in range(3):
                head = 3 * g + h
                out[128 * b : 128 * b + 128, 64 * head : 64 * head + 64] = turned[
                    128 * h : 128 * h + 128
                ]


def attend(sc, q, kvs):
    return call(
        attend_kernel,
        (sc, q, kvs),
        [SM, VM, VM],
        (shaped((256, D), BF), shaped((6, 8, 384), F32)),
        [
            pltpu.VMEM((6, 384, 128), BF),
            pltpu.VMEM((6, 128, 384), BF),
            pltpu.VMEM((17, 128, 384), F32),
            pltpu.VMEM((128, 384), F32),
            pltpu.VMEM((6, HD, 384), F32),
        ],
        4 * 17 * 3 * 128 * 128 * 384,
        4_000_000,
    )


def attend_back_kernel(
    sc, q, rows_out, grad_out, log_total, cosine, sine, held, grad_q, grad_kv, both, delta, acc,
    early, slotted, dq, mask, probs, probs_low, grads_low, turned, turned_q, turned_g,
):
    fill_padded(both, q[...].astype(F32), 0, 0)
    fill_padded(both, grad_out[...].astype(F32), 384, 64)
    fill_turned(turned_q, both, 0)
    fill_turned(turned_g, both, 384)
    fill_mask(mask)
    product = rows_out[...].astype(F32) * grad_out[...].astype(F32)
    for g in range(KVH):
        for b in range(2):
            for h in range(3):
                head = 3 * g + h
                piece = product[128 * b : 128 * b + 128, 64 * head : 64 * head + 64]
                delta[2 * g + b, 0:1, 128 * h : 128 * h + 128] = jnp.sum(
                    piece.T, axis=0, keepdims=True
                )
    slots = slots_of(sc)

    def key_head(g, carry):
        lanes = pl.ds(pl.multiple_of(128 * g, 128), 128)
        for k, (is_low, block, masked) in enumerate(slots):
            at = 2 * g + pick(is_low, 0, 1)
            score = nn(held[block, :, lanes], turned_q[at])
            if masked is not None:
                score = score + mask[...] * masked
            prob = jnp.exp(score - log_total[at, 0:1])
            probs[k] = prob
            probs_low[k] = prob.astype(BF)
        for k, (is_low, block, _) in enumerate(slots):
            at = 2 * g + pick(is_low, 0, 1)
            tile = held[block, :, lanes]
            grad_prob = nn(tile, turned_g[at])
            grads_low[128 * k : 128 * k + 128] = (
                probs[k] * (grad_prob - delta[at, 0:1])
            ).astype(BF)
            turned[:, 128 * k : 128 * k + 128] = tile.astype(F32).T[:HD].astype(BF)
        low = jnp.zeros((HD, 384), F32)
        high = nn(turned[:, 1152:], grads_low[1152:])
        for k, (is_low, _, _) in enumerate(slots):
            at = 2 * g + pick(is_low, 0, 1)
            rows = slice(128 * k, 128 * k + 128)
            grad_score = grads_low[rows]
            if k < 9:
                low, high = add_to(is_low, low, high, nn(turned[:, rows], grad_score), jnp.add)
            pair = nn(grad_score, both[at, :384]) + nn(probs_low[k], both[at, 384:])
            if k < 9:
                slotted[k, :, lanes] = pair
            else:
                early[k - 9, :, lanes] = pair + jnp.where(
                    k - 9 <= sc[2], slotted[k - 9, :, lanes], 0.0
                )
        acc[2 * g] = low
        acc[2 * g + 1] = high
        return carry

    lax.fori_loop(0, KVH, key_head, 0)
    dq[...] = jnp.zeros_like(dq)
    for g in range(KVH):
        for b in range(2):
            heads = acc[2 * g + b].T
            for h in range(3):
                head = 3 * g + h
                dq[128 * b : 128 * b + 128, 64 * head : 64 * head + 64] = heads[
                    128 * h : 128 * h + 128
                ] * (HD**-0.5)
    turned = rope_back(
        dq[...], table_lanes(cosine[...], 1.0)[:, 384:], table_lanes(sine[...], 0.0)[:, 384:]
    )
    grad_q[...] = turned[:, :D].astype(BF)
    for r in range(8):
        pair = sc[13 + r]
        slot = 8 + sc[2] - pair
        grad_kv[2 * r] = early[pair].astype(BF)
        grad_kv[2 * r + 1] = jnp.where(
            slot <= 8, slotted[jnp.minimum(slot, 8)], 0.0
        ).astype(BF)


def attend_back(sc, q, rows_out, grad_out, log_total, tables, kvs):
    return call(
        attend_back_kernel,
        (sc, q, rows_out, grad_out, log_total, *tables, kvs),
        [SM] + [VM] * 7,
        (shaped((256, D), BF), shaped((16, 128, 384), BF)),
        [
            pltpu.VMEM((6, 768, 128), BF),
            pltpu.VMEM((6, 8, 384), F32),
            pltpu.VMEM((6, 64, 384), F32),
            pltpu.VMEM((8, 128, 384), F32),
            pltpu.VMEM((9, 128, 384), F32),
            pltpu.VMEM((256, 640), F32),
            pltpu.VMEM((128, 384), F32),
            pltpu.VMEM((17, 128, 384), F32),
            pltpu.VMEM((17, 128, 384), BF),
            pltpu.VMEM((17 * 128, 384), BF),
            pltpu.VMEM((HD, 17 * 128), BF),
            pltpu.VMEM((6, 128, 384), BF),
            pltpu.VMEM((6, 128, 384), BF),
        ],
        10 * 17 * 3 * 128 * 128 * 384,
        8_000_000,
    )


CHUNK = 512


def feed_kernel(x, rows_out, gain, copies, *refs):
    middle_out, normed_out, gate_out, up_out, after = refs[:5]
    weight, gate_w, up_w, down_w, _ = refs[5:]
    first, second, third = copies
    wait_all(first)
    middle = x[...] + nn(rows_out[...], weight[:, 960:])
    middle_out[...] = middle
    normed = (middle * norm_factor(middle) * gain[...]).astype(BF)
    normed_out[...] = normed
    wait_all(second)
    wait_all(third)
    total = middle
    for at in range(0, FF, CHUNK):
        gate = nn(normed, gate_w[:, at : at + CHUNK])
        up = nn(normed, up_w[:, at : at + CHUNK])
        gate_out[:, at : at + CHUNK] = gate
        up_out[:, at : at + CHUNK] = up
        hidden = (gate * jax.nn.sigmoid(gate) * up).astype(BF)
        total = total + nn(hidden, down_w[at : at + CHUNK, :D])
    after[...] = total


def feed(sc, x, rows_out, gain, c_pieces, m_pieces):
    c_pieces, m_pieces = c_pieces[0], m_pieces[0]
    n_m = len(m_pieces)

    def kernel(sc, x, rows_out, gain, *refs):
        c_refs, m_refs, refs = refs[:PIECES], refs[PIECES : PIECES + n_m], refs[PIECES + n_m :]
        copies = weight_copies(sc, c_refs, m_refs, refs[5:], False)
        feed_kernel(x, rows_out, gain, copies, *refs)

    wide = shaped((256, FF), F32)
    narrow = shaped((256, D), F32)
    return call(
        kernel,
        (sc, x, rows_out, gain, *c_pieces, *m_pieces),
        [SM] + [VM] * 3 + [ANY] * 2 * PIECES,
        (narrow, shaped((256, D), BF), wide, wide, narrow),
        [
            pltpu.VMEM((D, FF), BF),
            pltpu.VMEM((D, FF), BF),
            pltpu.VMEM((D, FF), BF),
            pltpu.VMEM((FF, HALF), BF),
            pltpu.SemaphoreType.DMA((32,)),
        ],
        2 * 256 * D * (D + 3 * FF),
        14_000_000,
    )


def weight_copies(sc, c_pieces, m_pieces, scratch, last_first):
    weight, gate_w, up_w, down_w, sems = scratch

    def square():
        return unit_copies(sc, c_pieces, 0, 144, weight, 144, False, sems, 0)

    first = None if last_first else square()
    third = unit_copies(sc, m_pieces, 288, 192, down_w, 384, True, sems, 24) if last_first else None
    second = unit_copies(sc, m_pieces, 0, 144, gate_w, 144, False, sems, 8)
    second += unit_copies(sc, m_pieces, 144, 144, up_w, 144, False, sems, 16)
    if third is None:
        third = unit_copies(sc, m_pieces, 288, 192, down_w, 384, True, sems, 24)
    return square() if first is None else first, second, third


def feed_back_kernel(upstream, middle, gate, up, gain, copies, *refs):
    grad_middle, grad_attn_out, grad_rows, grad_gate_out, grad_up_out, hidden_out, grad_gain = refs[
        :7
    ]
    weight, gate_w, up_w, down_w, _ = refs[7:]
    first, second, third = copies
    grad_down = upstream[...].astype(BF)
    wait_all(third)
    wait_all(second)
    grad_normed = jnp.zeros((256, D), F32)
    for at in range(0, FF, CHUNK):
        lanes = slice(at, at + CHUNK)
        grad_hidden = nt(grad_down, down_w[at : at + CHUNK, :D])
        gate_act, up_proj = gate[:, lanes], up[:, lanes]
        sigma = jax.nn.sigmoid(gate_act)
        silu = gate_act * sigma
        grad_gate = (grad_hidden * up_proj * sigma * (1.0 + gate_act * (1.0 - sigma))).astype(BF)
        grad_up = (grad_hidden * silu).astype(BF)
        grad_gate_out[:, lanes] = grad_gate
        grad_up_out[:, lanes] = grad_up
        hidden_out[:, lanes] = (silu * up_proj).astype(BF)
        grad_normed = grad_normed + nt(grad_gate, gate_w[:, lanes]) + nt(grad_up, up_w[:, lanes])
    back, grad_gain_sum = norm_back(middle[...], gain[...], grad_normed)
    grad_gain[...] = grad_gain_sum
    total = upstream[...] + back
    grad_middle[...] = total
    grad_attn = total.astype(BF)
    grad_attn_out[...] = grad_attn
    wait_all(first)
    grad_rows[...] = nt(grad_attn, weight[:, 960:]).astype(BF)


FEED_BACK_OUTS = (
    (shaped((256, D), F32),)
    + (shaped((256, D), BF),) * 2
    + (shaped((256, FF), BF),) * 3
    + (shaped((1, D), F32),)
)
FEED_SCRATCH = [pltpu.VMEM((D, FF), BF)] * 3 + [
    pltpu.VMEM((FF, HALF), BF),
    pltpu.SemaphoreType.DMA((32,)),
]


def feed_both(sc, x, rows_out, gain, upstream, c_pieces, m_pieces):
    c_pieces, m_pieces = c_pieces[0], m_pieces[0]
    n_m = len(m_pieces)

    def kernel(sc, x, rows_out, gain, upstream, *refs):
        c_refs, m_refs, refs = refs[:PIECES], refs[PIECES : PIECES + n_m], refs[PIECES + n_m :]
        mixed, normed_out, back_outs, refs = refs[0], refs[1], refs[2:9], refs[9:]
        middle, gate, up, after, *scratch = refs
        copies = weight_copies(sc, c_refs, m_refs, scratch, False)
        feed_kernel(
            x, rows_out, gain, copies, middle, normed_out, gate, up, after, *scratch
        )
        mixed[...] = after[...].T.astype(BF)
        feed_back_kernel(
            upstream, middle, gate, up, gain, ([], [], []), *back_outs, *scratch
        )

    return call(
        kernel,
        (sc, x, rows_out, gain, upstream, *c_pieces, *m_pieces),
        [SM] + [VM] * 4 + [ANY] * (PIECES + n_m),
        (shaped((D, 256), BF), shaped((256, D), BF)) + FEED_BACK_OUTS,
        [
            pltpu.VMEM((256, D), F32),
            pltpu.VMEM((256, FF), F32),
            pltpu.VMEM((256, FF), F32),
            pltpu.VMEM((256, D), F32),
        ]
        + FEED_SCRATCH,
        4 * 256 * D * (D + 3 * FF),
        14_000_000,
    )


def store_piece(sc, parts, owner, half, rows, value, own_first=True):
    slot = lax.rem(owner - sc[0] + 4, 4) if own_first else owner
    parts[jnp.where(sc[1] == half, 0, 1), slot, rows] = value


def send_parts(parts, keep, send, sems):
    copies = [
        pltpu.make_async_copy(parts.at[k], ref, sems.at[k]) for k, ref in enumerate((keep, send))
    ]
    for copy in copies:
        copy.start()
    wait_all(copies)


def parts_scratch(rows):
    return [pltpu.VMEM((2, 4, rows, HALF), BF), pltpu.SemaphoreType.DMA((2,))]


def feed_grads_kernel(sc, normed, grad_gate, grad_up, hidden, upstream, keep, send, turned, tall, *held):
    turned[...] = normed[...].astype(F32).T.astype(BF)
    for at in range(0, FF, CHUNK):
        tall[at : at + CHUNK] = hidden[:, at : at + CHUNK].astype(F32).T.astype(BF)
    grad_down = jnp.concatenate(
        [upstream[...], jnp.zeros((256, HALF - D), F32)], axis=1
    ).astype(BF)
    for half in range(2):
        lanes = slice(HALF * half, HALF * half + HALF)
        for owner in range(4):
            left = turned[144 * owner : 144 * owner + 144]
            at = 384 * owner + 192 * half
            for rows, value in (
                (slice(0, 144), nn(left, grad_gate[:, lanes])),
                (slice(144, 288), nn(left, grad_up[:, lanes])),
                (slice(288, 480), nn(tall[at : at + 192], grad_down)),
            ):
                store_piece(sc, held[0], owner, half, rows, value.astype(BF))
    send_parts(held[0], keep, send, held[1])


def feed_grads(sc, normed, grad_gate, grad_up, hidden, upstream):
    out = shaped((4, MROWS, HALF), BF)
    return call(
        feed_grads_kernel,
        (sc, normed, grad_gate, grad_up, hidden, upstream),
        [SM] + [VM] * 5,
        (out, out),
        [pltpu.VMEM((D, 256), BF), pltpu.VMEM((FF, 256), BF)] + parts_scratch(MROWS),
        2 * 256 * D * 3 * FF,
        9_000_000,
        2,
    )


def grad_kv_rows(grad_kvs, cosine, sine, half):
    total = grad_kvs[0, half].astype(F32)
    for r in range(1, 8):
        total = total + grad_kvs[r, half].astype(F32)
    rows = slice(128 * half, 128 * half + 128)
    cos_t, sin_t = table_lanes(cosine[rows], 1.0), table_lanes(sine[rows], 0.0)
    return rope_back(total, cos_t[:, :384], sin_t[:, :384])


def project_back_kernel(
    sc, x, gain, cosine, sine, grad_middle, grad_q, normed, attn_rows, grad_attn, gain_two,
    grad_kvs, *refs,
):
    pieces, (upstream, keep, send, weight, buf, turned, sems, *held) = (
        refs[:PIECES], refs[PIECES:]
    )
    copies = unit_copies(sc, pieces, 0, 144, weight, 144, False, sems, 0)
    for half in range(2):
        rows = slice(128 * half, 128 * half + 128)
        buf[rows, :384] = grad_kv_rows(grad_kvs, cosine, sine, half)
    buf[:, 384:960] = grad_q[...].astype(F32)
    buf[:, 960:] = grad_attn[...].astype(F32)
    inner = buf[:, :960].astype(BF)
    wait_all(copies)
    grad_normed = nt(inner, weight[:, :960])
    back, grad_gain = norm_back(x[...], gain[...], grad_normed)
    upstream[...] = grad_middle[...] + back
    turned[0] = normed[...].astype(F32).T.astype(BF)
    turned[1] = attn_rows[...].astype(F32).T.astype(BF)
    right = [buf[:, :HALF].astype(BF), buf[:, HALF:].astype(BF)]
    lane = lax.broadcasted_iota(jnp.int32, (144, HALF), 1)
    gains = (grad_gain, gain_two[...])
    for owner in range(4):
        rows = slice(144 * owner, 144 * owner + 144)
        for half in range(2):
            value = nn(turned[0, rows], right[half])
            if half == 1:
                value = jnp.where(lane < 192, value, nn(turned[1, rows], right[1]))
            store_piece(sc, held[0], owner, half, slice(0, 144), value.astype(BF), False)
            row = jnp.concatenate([gains[half][:, rows], jnp.zeros((1, HALF - 144), F32)], axis=1)
            block = jnp.broadcast_to(row, (16, HALF))
            store_piece(sc, held[0], owner, half, slice(144, 160), block.astype(BF), False)
    send_parts(held[0], keep, send, held[1])


def between_layers(
    sc, x, gain, tables, grad_middle, grad_q, normed, attn_rows, grad_attn, gain_two, grad_kvs,
    pieces, middle, gate, up, gain_below, c_pieces, m_pieces,
):
    pieces, c_pieces, m_pieces = pieces[0], c_pieces[0], m_pieces[0]
    n_m = len(m_pieces)

    def kernel(sc, *refs):
        ins, refs = refs[:11], refs[11:]
        below, refs = refs[:4], refs[4:]
        mine, c_refs, refs = refs[:PIECES], refs[PIECES : 2 * PIECES], refs[2 * PIECES :]
        m_refs, refs = refs[:n_m], refs[n_m:]
        upstream, back_outs, keep, send, refs = refs[0], refs[1:8], refs[8], refs[9], refs[10:]
        scratch = refs[6:]
        copies = weight_copies(sc, c_refs, m_refs, scratch, True)
        project_back_kernel(sc, *ins, *mine, upstream, keep, send, *refs[:6])
        feed_back_kernel(upstream, *below, copies, *back_outs, *scratch)

    out = shaped((4, CROWS, HALF), BF)
    return call(
        kernel,
        (
            sc, x, gain, *tables, grad_middle, grad_q, normed, attn_rows, grad_attn, gain_two,
            grad_kvs, middle, gate, up, gain_below, *pieces, *c_pieces, *m_pieces,
        ),
        [SM] + [VM] * 15 + [ANY] * (2 * PIECES + n_m),
        (shaped((256, D), F32),) + FEED_BACK_OUTS + (out, out),
        [
            pltpu.VMEM((D, FF), BF),
            pltpu.VMEM((256, FF), F32),
            pltpu.VMEM((2, D, 256), BF),
            pltpu.SemaphoreType.DMA((8,)),
        ]
        + parts_scratch(CROWS)
        + FEED_SCRATCH,
        2 * 256 * D * (960 + 2 * FF),
        20_000_000,
        2,
    )


def early_grads_kernel(sc, normed, grad_q, attn_rows, grad_attn, keep, send, turned, *held):
    turned[0] = normed[...].astype(F32).T.astype(BF)
    turned[1] = attn_rows[...].astype(F32).T.astype(BF)
    for half, right in enumerate((grad_q, grad_attn)):
        for owner in range(4):
            value = nn(turned[half, 144 * owner : 144 * owner + 144], right[...])
            value = jnp.concatenate([value, jnp.zeros((144, HALF - D), F32)], axis=1)
            value = jnp.concatenate([value, jnp.zeros((16, HALF), F32)], axis=0)
            store_piece(sc, held[0], owner, half, slice(0, CROWS), value.astype(BF))
    send_parts(held[0], keep, send, held[1])


def early_grads(sc, normed, grad_q, attn_rows, grad_attn):
    out = shaped((4, CROWS, HALF), BF)
    return call(
        early_grads_kernel,
        (sc, normed, grad_q, attn_rows, grad_attn),
        [SM] + [VM] * 4,
        (out, out),
        [pltpu.VMEM((2, D, 256), BF)] + parts_scratch(CROWS),
        4 * 256 * D * D,
        4_000_000,
        2,
    )


LROWS = 80


def late_back_kernel(
    at, sc, x, gain, cosine, sine, grad_middle, grad_q, normed, gain_two, grad_kvs, *refs
):
    pieces, (grad_tokens, parts, weight, buf, turned, sems) = refs[:PIECES], refs[PIECES:]
    copies = unit_copies(sc, pieces, at, 144, weight, 144, False, sems, 0)
    for half in range(2):
        rows = slice(128 * half, 128 * half + 128)
        buf[rows, :384] = grad_kv_rows(grad_kvs, cosine, sine, half).astype(BF)
    buf[:, 384:] = grad_q[...]
    wait_all(copies)
    grad_normed = nt(buf[...], weight[:, :960])
    back, grad_gain = norm_back(x[...], gain[...], grad_normed)
    grad_tokens[...] = (grad_middle[...] + back).T.astype(BF)
    turned[...] = normed[...].astype(F32).T.astype(BF)
    gains = (grad_gain, gain_two[...])
    for owner in range(4):
        rows = slice(144 * owner, 144 * owner + 144)
        value = nn(turned[rows], buf[:, :384])
        for half in range(2):
            row = jnp.concatenate([gains[half][:, rows], jnp.zeros((1, 384 - 144), F32)], axis=1)
            block = jnp.broadcast_to(row, (8, 384))
            piece = jnp.concatenate([value[72 * half : 72 * half + 72], block], axis=0)
            parts[4 * half + owner] = piece.astype(BF)


def late_back(sc, x, gain, tables, grad_middle, grad_q, normed, gain_two, grad_kvs, pieces):
    pieces, at = pieces

    def kernel(*refs):
        late_back_kernel(at, *refs)

    return call(
        kernel,
        (sc, x, gain, *tables, grad_middle, grad_q, normed, gain_two, grad_kvs, *pieces),
        [SM] + [VM] * 9 + [ANY] * PIECES,
        (shaped((D, 256), BF), shaped((8, LROWS, 384), BF)),
        [
            pltpu.VMEM((D, FF), BF),
            pltpu.VMEM((256, 960), BF),
            pltpu.VMEM((D, 256), BF),
            pltpu.SemaphoreType.DMA((8,)),
        ],
        2 * 256 * D * (960 + 384),
        6_000_000,
    )


def halves_in_order(sc, mine, other):
    rows = mine[...].astype(F32), other[...].astype(F32)
    is_first = sc[1] == 0
    return jnp.where(is_first, rows[0], rows[1]), jnp.where(is_first, rows[1], rows[0])


def in_order(sc, mine, other, spread):
    first = MROWS // 4
    second = mine.shape[1] - first
    for k in range(4):
        slot = lax.rem(sc[12] + k, 4)
        at_first = pl.ds(pl.multiple_of(slot * first, 8), first)
        at_second = pl.ds(pl.multiple_of(MROWS + slot * second, 8), second)
        for side, ref in enumerate((mine, other)):
            spread[side, at_first] = ref[k, :first].astype(F32)
            spread[side, at_second] = ref[k, first:].astype(F32)
    return spread.at[sc[1]], spread.at[1 - sc[1]]


def heads_apart(rows):
    keys = [rows[:, 128 * g : 128 * g + HD] for g in range(KVH)]
    values = [rows[:, 128 * g + HD : 128 * g + 128] for g in range(KVH)]
    return jnp.concatenate(keys, axis=1), jnp.concatenate(values, axis=1)


def place_all(pairs, sems, layer):
    copies = [
        pltpu.make_async_copy(src, dst.at[layer], sems.at[k]) for k, (src, dst) in enumerate(pairs)
    ]
    for copy in copies:
        copy.start()
    return copies


def fill_wide(left, right, at, gate, up, down):
    for k, rows in enumerate((left, right)):
        lanes = slice(HALF * k, HALF * k + HALF)
        gate[:, lanes] = rows[at : at + 144]
        up[:, lanes] = rows[at + 144 : at + 288]
    halves = [rows[at + 288 : at + 480, :D] for rows in (left, right)]
    down[...] = jnp.concatenate(halves, axis=0).T


def fill_square(left, right, at, query, out, key, value):
    query[:, :384], query[:, 384:] = left[at : at + 144, 384:], right[at : at + 144, :192]
    out[...] = right[at : at + 144, 192:]
    key[...], value[...] = heads_apart(left[at : at + 144, :384])


def assemble_kernel(sc, mine, other, e_mine, e_other, l_mine, l_other, *refs):
    (gain_a, gain_b), outs, held, spread, sems = refs[:2], refs[2:9], refs[9:23], refs[23], refs[24]
    left, right = in_order(sc, mine, other, spread)
    fill_wide(left, right, 0, *held[:3])
    copies = place_all(zip(held[:3], outs[:3]), sems, 1)
    fill_wide(left, right, MROWS + CROWS, *held[3:6])
    copies += place_all(zip(held[3:6], outs[:3]), sems.at[pl.ds(3, 3)], 0)
    fill_square(left, right, MROWS, *held[6:10])
    copies += place_all(zip(held[6:10], outs[3:]), sems.at[pl.ds(6, 4)], 1)
    row = MROWS + 144
    gain_a[1:2], gain_b[1:2] = left[row : row + 1, :144], right[row : row + 1, :144]
    query, out, key, value = held[10:]
    left, right = halves_in_order(sc, e_mine, e_other)
    query[...], out[...] = left[:144, :D], right[:144, :D]
    left, right = halves_in_order(sc, l_mine, l_other)
    key[...], value[...] = heads_apart(jnp.concatenate([left[:72], right[:72]], axis=0))
    gain_a[0:1], gain_b[0:1] = left[72:73, :144], right[72:73, :144]
    copies += place_all(zip(held[10:], outs[3:]), sems.at[pl.ds(10, 4)], 0)
    wait_all(copies)


PLACED = ((144, FF),) * 2 + ((D, 384),) + ((144, D),) * 2 + ((144, KVH * HD),) * 2


def assemble(*ins):
    held = PLACED[:3] + PLACED[:3] + PLACED[3:] + PLACED[3:]
    return pl.pallas_call(
        assemble_kernel,
        out_shape=(shaped((LAYERS, 144), F32),) * 2
        + tuple(shaped((LAYERS,) + shape, F32) for shape in PLACED),
        in_specs=[SM] + [VM] * (len(ins) - 1),
        out_specs=[VM] * 2 + [ANY] * len(PLACED),
        scratch_shapes=[pltpu.VMEM(shape, F32) for shape in held]
        + [
            pltpu.VMEM((2, 4 * ins[1].shape[1], HALF), F32),
            pltpu.SemaphoreType.DMA((len(held),)),
        ],
        compiler_params=pltpu.CompilerParams(vmem_limit_bytes=VMEM_LIMIT),
        cost_estimate=pl.CostEstimate(flops=1000, bytes_accessed=1000, transcendentals=0),
    )(*ins)


def ring(axis, shift):
    n = lax.axis_size(axis)
    return [(i, (i + shift) % n) for i in range(n)]


def swap_core(value):
    return lax.ppermute(value, "core", [(0, 1), (1, 0)])


def all_pairs(value, axis):
    return lax.all_to_all(value, axis, 0, 0, tiled=True)


def copied(value, n):
    return jnp.broadcast_to(value[None], (n,) + value.shape)


def added(parts):
    total = parts[0].astype(F32)
    for part in parts[1:]:
        total = total + part.astype(F32)
    return total


def summed_rows(pieces, n):
    return added([pieces[k] for k in range(n)])


def around(own, axis):
    own = own.astype(BF)
    return added([own] + [lax.ppermute(own, axis, ring(axis, s)) for s in (1, 2, 3)])


def phase(*values):
    return lax.optimization_barrier(values)


def sent(pieces, shifts):
    return [lax.ppermute(pieces[k], "fsdp", ring("fsdp", k)) for k in shifts]


def near(mine, shifts):
    return [lax.ppermute(mine, "fsdp", ring("fsdp", -k)) for k in shifts]


def gathered(quarter, shifts):
    return [lax.ppermute(quarter, "dp", ring("dp", -k)) for k in shifts]


def swap_all(parts):
    return [swap_core(part) for part in parts]


def joined(parts):
    return [
        jnp.concatenate([added([keep[k], got[k]]).astype(BF) for keep, got in parts], axis=0)
        for k in range(4)
    ]


def quarters(total):
    return total.astype(BF).reshape(4, -1, HALF)


def halves_of(full):
    return jnp.stack([full[:, :HALF], full[:, HALF:]])


def of_core(own, core):
    return lax.dynamic_index_in_dim(own, core, 0, keepdims=False)


def local(
    tokens, pair_order, cotangent, norm_first, w_query, w_key, w_value, w_out, norm_second,
    w_gate, w_up, w_down,
):
    core = lax.axis_index("core")
    rank = lax.axis_index("x") * 2 + core
    y = lax.axis_index("fsdp")
    order = pair_order[0]
    my_pair = lax.dynamic_index_in_dim(order, rank, 0, keepdims=False)
    ids = jnp.arange(8, dtype=jnp.int32)
    inverse = jnp.sum(jnp.where(order[None, :] == ids[:, None], ids[None, :], 0), axis=1)
    sc = jnp.concatenate(
        [
            jnp.stack([y, core, my_pair, rank]).astype(jnp.int32),
            inverse.astype(jnp.int32),
            lax.axis_index("dp").astype(jnp.int32)[None],
            order.astype(jnp.int32),
        ]
    )

    offsets = jnp.arange(256, dtype=jnp.int32)
    pos = jnp.where(
        offsets < 128, my_pair * 128 + offsets, (15 - my_pair) * 128 + offsets - 128
    )
    freq = jnp.power(THETA, -2.0 * (jnp.arange(128) % 32).astype(F32) / HD)
    angle = pos.astype(F32)[:, None] * freq
    tables = (jnp.cos(angle), jnp.sin(angle))

    gain_rows = jnp.pad(
        jnp.stack([norm_first[0], norm_second[0], norm_first[1], norm_second[1]]),
        ((0, 12), (0, HALF - 144)),
    )
    def c_slices(layer):
        cols = []
        for g in range(KVH):
            cols += [w_key[layer][:, 64 * g : 64 * g + 64], w_value[layer][:, 64 * g : 64 * g + 64]]
        full = jnp.concatenate(cols + [w_query[layer], w_out[layer]], axis=1)
        return jnp.concatenate(
            [halves_of(full), jnp.broadcast_to(gain_rows, (2, 16, HALF))], axis=1
        )

    def m_slices(gate, up, down):
        down = jnp.pad(down.reshape(2, 192, D), ((0, 0), (0, 0), (0, HALF - D)))
        return jnp.concatenate([halves_of(gate), halves_of(up), down], axis=1)

    own_c = c_slices(0)
    mine_c = of_core(own_c, core)
    own_b = m_slices(w_gate[0], w_up[0], w_down[0])
    mine_b = of_core(own_b, core)
    near_c = near(mine_c, (1, 2, 3))
    far_c = swap_all(near_c)
    gains = jnp.stack([mine_c[144:148, :144]] + [part[144:148, :144] for part in near_c])
    gains = jnp.roll(gains, y, axis=0).transpose(1, 0, 2).reshape(4, 1, D).astype(F32)
    gain_one, gain_two = (gains[0], gains[2]), (gains[1], gains[3])
    c_zero = ((own_c, *near_c, *far_c), 0)

    x = tokens[0].astype(F32)
    b1, b3 = near(mine_b, (1, 3))
    kv, q, normed = project(sc, x, gain_one[0], tables, c_zero)
    kv, *late_w = phase(kv, w_gate[1], w_up[1], w_down[1])
    (b2,) = near(mine_b, (2,))
    f1, f3 = swap_all((b1, b3))
    kvs = all_pairs(kv, ("x", "core")).reshape(16, 128, 384)
    own_d, own_m = c_slices(1), m_slices(*late_w)
    mine_d, mine_m = of_core(own_d, core), of_core(own_m, core)
    kvs, b2, f1, f3, mine_d, own_d, mine_m, own_m = phase(
        kvs, b2, f1, f3, mine_d, own_d, mine_m, own_m
    )
    f2 = swap_core(b2)
    near_d = near(mine_d, (1, 2, 3))
    rows_out, log_total = attend(sc, q, kvs)
    rows_out, f2, mine_m, *near_d = phase(rows_out, f2, mine_m, *near_d)
    m_zero = ((own_b, b1, b2, b3, f1, f2, f3), 0)
    c_one = ((own_d, *near_d, *swap_all(near_d)), 0)
    m1, m3 = near(mine_m, (1, 3))
    middle, normed_two, gate, up, after = feed(sc, x, rows_out, gain_two[0], c_zero, m_zero)
    saved = [(x, kvs, q, normed, rows_out, log_total, middle, normed_two, gate, up)]

    x = after
    kv, q, normed = project(sc, x, gain_one[1], tables, c_one)
    kv, m1, m3, mine_m = phase(kv, m1, m3, mine_m)
    (m2,) = near(mine_m, (2,))
    f1, f3 = swap_all((m1, m3))
    kvs = all_pairs(kv, ("x", "core")).reshape(16, 128, 384)
    kvs, m2, f1, f3 = phase(kvs, m2, f1, f3)
    f2 = swap_core(m2)
    rows_out, log_total = attend(sc, q, kvs)
    m_one = ((own_m, m1, m2, m3, f1, f2, f3), 0)
    upstream = cotangent[0].astype(F32)
    (
        mixed, normed_two, grad_middle, grad_attn, grad_rows, grad_gate, grad_up, hidden,
        grad_gain_two,
    ) = feed_both(sc, x, rows_out, gain_two[1], upstream, c_one, m_one)

    keep_m, send_m = feed_grads(sc, normed_two, grad_gate, grad_up, hidden, upstream)
    grad_rows, send_m = phase(grad_rows, send_m)
    got_m = swap_core(send_m)
    grad_q, grad_kvs = attend_back(sc, q, rows_out, grad_rows, log_total, tables, kvs)
    last = joined([(keep_m, got_m)])
    grad_kvs, *last = phase(grad_kvs, *last)
    l1, l3 = sent(last, (1, 3))
    grad_kvs = all_pairs(grad_kvs.reshape(8, 2, 128, 384), ("x", "core"))
    grad_kvs, l1, l3, *last = phase(grad_kvs, l1, l3, *last)
    (l2,) = sent(last, (2,))
    x_one, q_one, normed_one, rows_one = x, q, normed, rows_out
    x, kvs, q, normed, rows_out, log_total, middle, normed_two, gate, up = saved[0]
    (
        upstream, grad_middle, grad_attn, grad_rows, grad_gate, grad_up, hidden, grad_gain_two,
        keep_c, send_c,
    ) = between_layers(
        sc, x_one, gain_one[1], tables, grad_middle, grad_q, normed_one, rows_one, grad_attn,
        grad_gain_two, grad_kvs, c_one, middle, gate, up, gain_two[0], c_zero, m_zero,
    )

    last = quarters(added([last[0], l1, l2, l3]))
    grad_gate, send_c, last = phase(grad_gate, send_c, last)
    last = all_pairs(last, "dp")
    got_c = swap_core(send_c)
    keep_m, send_m = feed_grads(sc, normed_two, grad_gate, grad_up, hidden, upstream)
    last = summed_rows(last, 4)
    grad_rows, send_m, last, got_c = phase(grad_rows, send_m, last, got_c)
    middle_c = all_pairs(added([keep_c, got_c]).astype(BF), "fsdp")
    got_m = swap_core(send_m)
    last = around(last, "x").astype(BF)
    grad_q, grad_kvs = attend_back(sc, q, rows_out, grad_rows, log_total, tables, kvs)
    first = joined([(keep_m, got_m)])
    grad_kvs, grad_q, last, middle_c, *first = phase(grad_kvs, grad_q, last, middle_c, *first)
    f1, f2, f3 = sent(first, (1, 2, 3))
    (a2,) = gathered(last, (2,))
    grad_kvs = all_pairs(grad_kvs.reshape(8, 2, 128, 384), ("x", "core"))
    keep_e, send_e = early_grads(sc, normed, grad_q, rows_out, grad_attn)
    early = joined([(keep_e, swap_core(send_e))])
    first = quarters(
        jnp.concatenate([summed_rows(middle_c, 4), added([first[0], f1, f2, f3])], axis=0)
    )
    grad_kvs, first, last, a2, *early = phase(grad_kvs, first, last, a2, *early)
    first = all_pairs(first, "dp")
    a1, a3 = gathered(last, (1, 3))
    e1, e2, e3 = sent(early, (1, 2, 3))
    grad_tokens, late = late_back(
        sc, x, gain_one[0], tables, grad_middle, grad_q, normed, grad_gain_two, grad_kvs, c_zero
    )

    early = added([early[0], e1, e2, e3]).astype(BF)
    first = summed_rows(first, 4).astype(BF)
    late, first, early, a1, a3 = phase(late, first, early, a1, a3)
    late = summed_rows(all_pairs(late, ("core", "fsdp")), 8).astype(BF)
    first = around(first, "x").astype(BF)
    early = around(early, "dp").astype(BF)
    late, first, early = phase(late, first, early)
    joint = jnp.concatenate([early, late.reshape(LROWS // 2, HALF)], axis=0)
    joint = summed_rows(all_pairs(copied(joint, 4), "x"), 4).astype(BF)
    b1, b2, b3 = gathered(first, (1, 2, 3))
    first = jnp.concatenate(
        [jnp.stack([last, a1, a2, a3]), jnp.stack([first, b1, b2, b3])], axis=1
    )
    joint, first = phase(joint, first)
    early, late = joint[:CROWS], joint[CROWS:]
    late = around(late, "dp").astype(BF)
    first, early = (first, swap_core(first)), (early, swap_core(early))
    late, first, early = phase(late, first, early)
    late = late.reshape(LROWS, 384)
    gain_a, gain_b, gate, up, down, query, out, key, value = assemble(
        sc, *first, *early, late, swap_core(late)
    )
    return (
        mixed.T[None], grad_tokens.T[None], gain_a, query, key, value, out, gain_b, gate, up,
        down.transpose(0, 2, 1),
    )


def solution(mesh):
    split = jax.sharding.Mesh(mesh.devices.reshape(4, 4, 2, 4), ("dp", "x", "core", "fsdp"))
    rows = P(("dp", "fsdp"), ("x", "core"), None)
    flat, deep = P(None, "fsdp"), P(None, "fsdp", None)
    return jax.shard_map(
        local,
        mesh=split,
        in_specs=(rows, P(("dp", "fsdp"), None), rows, flat) + (deep,) * 4 + (flat,) + (deep,) * 3,
        out_specs=(rows, rows, flat) + (deep,) * 4 + (flat,) + (deep,) * 3,
        check_vma=False,
    )
```
